32 devices in a mesh: rows: 8 (over y, x, core), seq: 4 (over z).
Axes of the slice: x: 2, y: 2, z: 4, core: 2. Of those that a mesh axis runs over, the one named last changes fastest.
Arguments:
- inputs: bfloat16 [8, 1024, 512], P('rows', 'seq'), may hold values from -6 to 6
- memory: bfloat16 [8, 1024, 1024], P('rows', 'seq'), may hold values from -6 to 6
- target_segments: int32 [8, 1024], P('rows', 'seq'), may hold values from 0 to 4, as said below
- memory_segments: int32 [8, 1024], P('rows', 'seq'), may hold values from 0 to 4, as said below
- self_project: bfloat16 [512, 1536], replicated, may hold values from -0.25 to 0.25
- self_query_bias: float32 [512], replicated, may hold values from -1.5 to 1.5
- self_value_bias: float32 [512], replicated, may hold values from -1 to 1
- self_output: bfloat16 [512, 512], replicated, may hold values from -0.5 to 0.5
- self_output_bias: float32 [512], replicated, may hold values from -1.5 to 1.5
- self_norm_gain: float32 [512], replicated, may hold values from 0.5 to 1.5
- self_norm_bias: float32 [512], replicated, may hold values from -1.5 to 1.5
- cross_query: bfloat16 [512, 512], replicated, may hold values from -0.25 to 0.25
- cross_query_bias: float32 [512], replicated, may hold values from -1.5 to 1.5
- cross_output: bfloat16 [512, 512], replicated, may hold values from -0.5 to 0.5
- cross_output_bias: float32 [512], replicated, may hold values from -1.5 to 1.5
- cross_norm_gain: float32 [512], replicated, may hold values from 0.5 to 1.5
- cross_norm_bias: float32 [512], replicated, may hold values from -1.5 to 1.5
- expand_weight: bfloat16 [512, 2048], replicated, may hold values from -0.25 to 0.25
- expand_bias: float32 [2048], replicated, may hold values from -1.5 to 1.5
- contract_weight: bfloat16 [2048, 512], replicated, may hold values from -0.25 to 0.25
- contract_bias: float32 [512], replicated, may hold values from -1.5 to 1.5
- final_norm_gain: float32 [512], replicated, may hold values from 0.5 to 1.5
- final_norm_bias: float32 [512], replicated, may hold values from -1.5 to 1.5
- cotangent: bfloat16 [8, 1024, 512], P('rows', 'seq'), may hold values from -16 to 16
Outputs:
- output: bfloat16 [8, 1024, 512], P('rows', 'seq')
- input_gradient: bfloat16 [8, 1024, 512], P('rows', 'seq')
- memory_gradient: bfloat16 [8, 1024, 1024], P('rows', 'seq')
- gradient_self_project: float32 [512, 1536], replicated
- gradient_self_query_bias: float32 [512], replicated
- gradient_self_value_bias: float32 [512], replicated
- gradient_self_output: float32 [512, 512], replicated
- gradient_self_output_bias: float32 [512], replicated
- gradient_self_norm_gain: float32 [512], replicated
- gradient_self_norm_bias: float32 [512], replicated
- gradient_cross_query: float32 [512, 512], replicated
- gradient_cross_query_bias: float32 [512], replicated
- gradient_cross_output: float32 [512, 512], replicated
- gradient_cross_output_bias: float32 [512], replicated
- gradient_cross_norm_gain: float32 [512], replicated
- gradient_cross_norm_bias: float32 [512], replicated
- gradient_expand_weight: float32 [512, 2048], replicated
- gradient_expand_bias: float32 [2048], replicated
- gradient_contract_weight: float32 [2048, 512], replicated
- gradient_contract_bias: float32 [512], replicated
- gradient_final_norm_gain: float32 [512], replicated
- gradient_final_norm_bias: float32 [512], replicated
The draws below stay inside these ranges and needn't reach their ends.
Inputs may be any that keep to these rules, and one draw needn't show every extreme that they name: `target_segments`: along each row the numbers never fall; every number of a row's target tokens also labels some of that row's memory tokens; in every row one document holds target positions below 256 and at or above 768. `memory_segments`: along each row the numbers never fall; a row's memory tokens carry exactly the numbers of its target tokens; in every row one document holds memory positions below 256 and at or above 768.
All inputs are finite; a program needn't handle non-finite values.
Results may differ from the reference program's by a relative error of at most 0.025.
Values may be sent and summed in bfloat16 or wider, within the bound.
No kernel may reach another device: no remote copies, remote signals or barrier semaphores. Data moves between devices by JAX's collectives and lax.ppermute only.
A program may use at most 128 MiB of HBM per device.

```python
import jax
import jax.numpy as jnp
from jax import lax

D = 512
HEADS = 8
HEAD_DIM = 64
FF = 2048
ROW_LEN = 1024
SEQ_DEV = 256
ROWS = 8
N_SEQ = 4


def segment_plan(key):
    lead_key, trail_key = jax.random.split(key)
    places = jnp.arange(ROWS)
    leading = jnp.where(places == 0, 1, jax.random.randint(lead_key, (ROWS,), 0, 2))
    trailing = jnp.where(places == 0, 1, jax.random.randint(trail_key, (ROWS,), 0, 2))
    return (leading, trailing)


def segment_labels(key, leading, trailing):
    keys = jax.random.split(key, 4)
    opening = jax.random.randint(keys[0], (ROWS,), 2, SEQ_DEV)
    closing = jax.random.randint(keys[1], (ROWS,), (N_SEQ - 1) * SEQ_DEV + 1, ROW_LEN - 1)
    before = jnp.where(leading == 1, jax.random.randint(keys[2], (ROWS,), 1, opening), 0)
    after = jnp.where(trailing == 1, jax.random.randint(keys[3], (ROWS,), closing + 1, ROW_LEN), ROW_LEN)
    places = jnp.arange(ROW_LEN)[None, :]
    labels = (places >= before[:, None]).astype(jnp.int32)
    labels = labels + (places >= opening[:, None]).astype(jnp.int32)
    labels = labels + (places >= closing[:, None]).astype(jnp.int32)
    labels = labels + (places >= after[:, None]).astype(jnp.int32)
    return labels


def draw_target_segments(key, part):
    leading, trailing = segment_plan(key)
    key = jax.random.fold_in(key, 11)
    return segment_labels(key, leading, trailing)


def draw_memory_segments(key, part):
    leading, trailing = segment_plan(key)
    key = jax.random.fold_in(key, 23)
    return segment_labels(key, leading, trailing)


def steps_of(stream_key, dims, cuts, low, high):
    factor_of = 1.0
    for dim, blocks in cuts:
        steps = jax.random.uniform(jax.random.fold_in(jax.random.fold_in(stream_key, 6), dim), (blocks,), jnp.float32, low / len(cuts), high / len(cuts))
        factor_of = factor_of * jnp.repeat(jnp.exp(steps), dims[dim] // blocks).reshape((-1,) + (1,) * (len(dims) - 1 - dim))
    return factor_of


def gaussian(key, dims, deviation, limit, shards=(), kind=jnp.bfloat16):
    values = deviation * jax.random.normal(key, dims, jnp.float32)
    if shards:
        values = values * steps_of(key, dims, shards, -0.22, 0.18)
    return jnp.clip(values, -limit, limit).astype(kind)


def setup_inputs(seed: int = 0) -> dict:
    key_list = jax.random.split(jax.random.key(seed), 25)
    return {
        "inputs": gaussian(key_list[0], (ROWS, ROW_LEN, D), 1.0, 6.0, ((0, 8), (1, 4))),
        "memory": gaussian(key_list[1], (ROWS, ROW_LEN, 2 * D), 1.0, 6.0, ((0, 8), (1, 4))),
        "target_segments": draw_target_segments(jax.random.fold_in(key_list[24], 71), 0),
        "memory_segments": draw_memory_segments(jax.random.fold_in(key_list[24], 71), 0),
        "self_project": gaussian(key_list[4], (D, 3 * D), D ** -0.5, 0.25),
        "self_query_bias": gaussian(key_list[5], (D,), 0.3, 1.5, (), jnp.float32),
        "self_value_bias": gaussian(key_list[6], (D,), 0.2, 1.0, (), jnp.float32),
        "self_output": gaussian(key_list[7], (D, D), (D // 4) ** -0.5, 0.5),
        "self_output_bias": gaussian(key_list[8], (D,), 0.3, 1.5, (), jnp.float32),
        "self_norm_gain": jnp.clip(1.0 + 0.1 * jax.random.normal(key_list[9], (D,), jnp.float32), 0.5, 1.5),
        "self_norm_bias": gaussian(key_list[10], (D,), 0.3, 1.5, (), jnp.float32),
        "cross_query": gaussian(key_list[11], (D, D), D ** -0.5, 0.25),
        "cross_query_bias": gaussian(key_list[12], (D,), 0.3, 1.5, (), jnp.float32),
        "cross_output": gaussian(key_list[13], (D, D), (D // 4) ** -0.5, 0.5),
        "cross_output_bias": gaussian(key_list[14], (D,), 0.3, 1.5, (), jnp.float32),
        "cross_norm_gain": jnp.clip(1.0 + 0.1 * jax.random.normal(key_list[15], (D,), jnp.float32), 0.5, 1.5),
        "cross_norm_bias": gaussian(key_list[16], (D,), 0.3, 1.5, (), jnp.float32),
        "expand_weight": gaussian(key_list[17], (D, FF), D ** -0.5, 0.25),
        "expand_bias": gaussian(key_list[18], (FF,), 0.3, 1.5, (), jnp.float32),
        "contract_weight": gaussian(key_list[19], (FF, D), (FF // 4) ** -0.5, 0.25),
        "contract_bias": gaussian(key_list[20], (D,), 0.3, 1.5, (), jnp.float32),
        "final_norm_gain": jnp.clip(1.0 + 0.1 * jax.random.normal(key_list[21], (D,), jnp.float32), 0.5, 1.5),
        "final_norm_bias": gaussian(key_list[22], (D,), 0.3, 1.5, (), jnp.float32),
        "cotangent": gaussian(key_list[23], (ROWS, ROW_LEN, D), 4.0, 16.0, ((0, 8), (1, 4))),
    }


highest = lax.Precision.HIGHEST

@jax.custom_vjp
def low(v):
    return lax.optimization_barrier(v.astype(jnp.bfloat16)).astype(jnp.float32)

@jax.custom_vjp
def low_back(v):
    return v

def low_keep(v):
    return (low(v), None)

def low_pass(kept, grad):
    return (grad,)

def back_keep(v):
    return (v, None)

def back_low(kept, grad):
    return (low(grad),)
low.defvjp(low_keep, low_pass)
low_back.defvjp(back_keep, back_low)

def layer_norm(value, gain, shift):
    center = lax.optimization_barrier(jnp.mean(value, axis=-1, keepdims=True))
    centred = value - center
    spread = lax.optimization_barrier(jnp.mean(centred * centred, axis=-1, keepdims=True))
    return centred * lax.rsqrt(spread + 1e-05) * gain + shift

def attend(query, keys, values, allowed):
    length = query.shape[0]
    span = keys.shape[0]
    query_heads = query.reshape(length, HEADS, HEAD_DIM)
    key_heads = keys.reshape(span, HEADS, HEAD_DIM)
    value_heads = values.reshape(span, HEADS, HEAD_DIM)
    scores = low_back(jnp.einsum('qhe,khe->hqk', query_heads, key_heads, precision=highest) * HEAD_DIM ** (-0.5))
    scores = jnp.where(allowed[None], scores, -1e+30)
    peak = lax.optimization_barrier(jnp.max(scores, axis=-1, keepdims=True))
    raised = jnp.exp(scores - peak)
    weights = low(raised / lax.optimization_barrier(jnp.sum(raised, axis=-1, keepdims=True)))
    mixed = jnp.einsum('hqk,khe->qhe', weights, value_heads, precision=highest)
    return mixed.reshape(length, HEADS * HEAD_DIM)

def block_forward(inputs, memory, target_labels, memory_labels, weights):
    self_project, self_query_bias, self_value_bias, self_output, self_output_bias, self_norm_gain, self_norm_bias, cross_query, cross_query_bias, cross_output, cross_output_bias, cross_norm_gain, cross_norm_bias, expand_weight, expand_bias, contract_weight, contract_bias, final_norm_gain, final_norm_bias = weights
    places = jnp.arange(ROW_LEN)
    causal = (target_labels[:, None] == target_labels[None, :]) & (places[None, :] <= places[:, None])
    crossing = target_labels[:, None] == memory_labels[None, :]
    bias = jnp.concatenate([self_query_bias, jnp.zeros_like(self_query_bias), self_value_bias])
    projected = low(low_back(jnp.dot(inputs, self_project, precision=highest) + bias))
    mixed = low(low_back(attend(projected[:, :D], projected[:, D:2 * D], projected[:, 2 * D:], causal)))
    branch = low_back(jnp.dot(mixed, self_output, precision=highest) + self_output_bias)
    first = layer_norm(inputs + branch, self_norm_gain, self_norm_bias)
    asked = low(low_back(jnp.dot(low(first), cross_query, precision=highest) + cross_query_bias))
    crossed = low(low_back(attend(asked, memory[:, :D], memory[:, D:], crossing)))
    branch = low_back(jnp.dot(crossed, cross_output, precision=highest) + cross_output_bias)
    second = layer_norm(first + branch, cross_norm_gain, cross_norm_bias)
    inner = low_back(jnp.dot(low(second), expand_weight, precision=highest) + expand_bias)
    activated = low(jax.nn.silu(inner))
    branch = low_back(jnp.dot(activated, contract_weight, precision=highest) + contract_bias)
    return layer_norm(second + branch, final_norm_gain, final_norm_bias)

def reference(inputs, memory, target_segments, memory_segments, self_project, self_query_bias, self_value_bias, self_output, self_output_bias, self_norm_gain, self_norm_bias, cross_query, cross_query_bias, cross_output, cross_output_bias, cross_norm_gain, cross_norm_bias, expand_weight, expand_bias, contract_weight, contract_bias, final_norm_gain, final_norm_bias, cotangent):
    weights = tuple((value.astype(jnp.float32) for value in (self_project, self_query_bias, self_value_bias, self_output, self_output_bias, self_norm_gain, self_norm_bias, cross_query, cross_query_bias, cross_output, cross_output_bias, cross_norm_gain, cross_norm_bias, expand_weight, expand_bias, contract_weight, contract_bias, final_norm_gain, final_norm_bias)))

    def one_row(totals, row):
        row_inputs, row_memory, row_target, row_source, row_cotangent = row

        def forward(given_inputs, given_memory, given_weights):
            return block_forward(given_inputs, given_memory, row_target, row_source, given_weights)
        result, pullback = jax.vjp(forward, row_inputs.astype(jnp.float32), row_memory.astype(jnp.float32), weights)
        input_gradient, memory_gradient, weight_gradients = pullback(row_cotangent.astype(jnp.float32))
        totals = tuple((total + piece for total, piece in zip(totals, weight_gradients)))
        return (totals, (result.astype(jnp.bfloat16), input_gradient.astype(jnp.bfloat16), memory_gradient.astype(jnp.bfloat16)))
    zeros = tuple((jnp.zeros_like(value) for value in weights))
    totals, (output, input_gradient, memory_gradient) = lax.scan(one_row, zeros, (inputs, memory, target_segments, memory_segments, cotangent))
    return (output, input_gradient, memory_gradient, totals[0], totals[1], totals[2], totals[3], totals[4], totals[5], totals[6], totals[7], totals[8], totals[9], totals[10], totals[11], totals[12], totals[13], totals[14], totals[15], totals[16], totals[17], totals[18])
```

```python
import functools

import jax
import jax.numpy as jnp
from jax import lax
from jax.experimental import pallas as pl
from jax.experimental.pallas import tpu as pltpu
from jax.sharding import PartitionSpec as P

HEADS = 8
PAIR = 128
SMALL_ROWS = 16
masked_score = -1e30
epsilon = 1e-05
f32 = jnp.float32
bf16 = jnp.bfloat16
BOTH = ("rows", "seq")


def dot(left, right):
    return jnp.dot(left, right, preferred_element_type=f32)


def dot_nt(left, right):
    return lax.dot_general(left, right, (((1,), (1,)), ((), ())), preferred_element_type=f32)


def dot_tn(left, right):
    return lax.dot_general(left, right, (((0,), (0,)), ((), ())), preferred_element_type=f32)


def norm_forward(value, gain, shift):
    center = jnp.mean(value, axis=-1, keepdims=True)
    centred = value - center
    scale = lax.rsqrt(jnp.mean(centred * centred, axis=-1, keepdims=True) + epsilon)
    normed = centred * scale
    return normed * gain + shift, normed, scale


def norm_backward(incoming, normed, scale, gain):
    weighted = incoming * gain
    spread = weighted - jnp.mean(weighted, axis=-1, keepdims=True)
    spread = spread - normed * jnp.mean(weighted * normed, axis=-1, keepdims=True)
    return scale * spread, column_total(incoming * normed), column_total(incoming)


def column_total(value):
    return jnp.sum(value.astype(f32), axis=0, keepdims=True)


def head_lanes(shape, h):
    lane = lax.broadcasted_iota(jnp.int32, shape, 1)
    return (lane < 64) if h == 0 else (lane >= 64)


def only_head(value, h):
    return jnp.where(head_lanes(value.shape, h), value, jnp.zeros_like(value))


def flat_pairs(rows, seq, partner):
    return [(r * seq + z, partner(r, z)) for r in range(rows) for z in range(seq)]


def home_route(rows, seq):
    def partner(r, z):
        if (r & 1) == z // 2:
            return r * seq + z
        return (r ^ 1) * seq + (z ^ 2)

    return flat_pairs(rows, seq, partner)


def bit_orders(rows):
    count = rows.bit_length() - 2
    bits = [("r", 1 << (k + 1)) for k in range(count)]
    tail = [("z", 1), ("z", 2)]
    return bits + tail, bits[::-1] + tail


def step_route(rows, seq, k):
    orders = bit_orders(rows)

    def partner(r, z):
        kind, mask = orders[r & 1][k]
        return (r ^ mask) * seq + z if kind == "r" else r * seq + (z ^ mask)

    return flat_pairs(rows, seq, partner)


def low_number(rows, order, r, z):
    number = jnp.int32(0)
    for kind, mask in order:
        bit = jnp.where(((r if kind == "r" else z) & mask) != 0, 1, 0)
        number = number * 2 + bit
    return number


def send(value, route):
    return lax.ppermute(value, BOTH, route)


def taking(us):
    return pl.CostEstimate(
        flops=int(us * 1.15e9), bytes_accessed=int(us * 3.6e6), transcendentals=0
    )


class Lazy:
    def __init__(self, far, near, sem):
        self.copy, self.near, self.waiting = pltpu.make_async_copy(far, near, sem), near, True
        self.copy.start()

    @property
    def shape(self):
        return self.near.shape

    def __getitem__(self, index):
        if self.waiting:
            self.copy.wait()
            self.waiting = False
        return self.near[index]


TOKEN = jax.ShapeDtypeStruct((8, 128), f32)


def call(kernel, outs, args, scratch=(), lazy=(), out_specs=None, cost=None, after=(), limit=24):
    vmem = pl.BlockSpec(memory_space=pltpu.VMEM)
    smem = pl.BlockSpec(memory_space=pltpu.SMEM)
    hbm = pl.BlockSpec(memory_space=pltpu.HBM)
    count = len(args)
    lazy = sorted(lazy)

    def spec(i, arg):
        if i in lazy:
            return hbm
        return smem if arg.dtype == jnp.int32 and arg.ndim == 1 else vmem

    def inner(*refs):
        given = list(refs[:count])
        rest = refs[count + len(after) :]
        results, token, held = rest[: len(outs)], rest[len(outs)], rest[len(outs) + 1 :]
        near, held = held[: len(lazy)], held[len(lazy) :]
        if lazy:
            sems, held = held[0], held[1:]
            for k, i in enumerate(lazy):
                given[i] = Lazy(given[i], near[k], sems.at[k])
        kernel(*given, *results, *held)
        for i in lazy:
            if given[i].waiting:
                given[i].copy.wait()
        token[...] = jnp.zeros_like(token)

    spaces = [pltpu.VMEM(args[i].shape, args[i].dtype) for i in lazy]
    if lazy:
        spaces.append(pltpu.SemaphoreType.DMA((len(lazy),)))
    res = pl.pallas_call(
        inner,
        out_shape=list(outs) + [TOKEN],
        in_specs=[spec(i, a) for i, a in enumerate(args)] + [vmem] * len(after),
        out_specs=(out_specs if out_specs is not None else [vmem] * len(outs)) + [vmem],
        scratch_shapes=spaces + list(scratch),
        compiler_params=pltpu.CompilerParams(vmem_limit_bytes=limit * 1024 * 1024),
        cost_estimate=None if cost is None else taking(cost),
    )(*args, *after)
    return res[:-1], res[-1]


def mask_bias(bias, place, query_labels, key_labels, length, causal):
    asking = jnp.broadcast_to(query_labels, (length, length)).T
    for s in range(4):
        same = asking == key_labels[s]
        if causal:
            query = place * length + lax.broadcasted_iota(jnp.int32, (length, length), 0)
            key = (place ^ s) * length + lax.broadcasted_iota(jnp.int32, (length, length), 1)
            same = same & (key <= query)
        bias[:, s * length : (s + 1) * length] = jnp.where(same, 0.0, masked_score)


def attend(query, keys, values, bias, factor, result, logs):
    length, width = query.shape
    lane = lax.broadcasted_iota(jnp.int32, (length, PAIR), 1)
    log_all = jnp.zeros((length, PAIR), f32)
    for j in range(width // PAIR):
        columns = slice(j * PAIR, (j + 1) * PAIR)
        pair = query[:, columns] * jnp.asarray(factor, bf16)
        key, value = keys(j), values(j)
        halves = []
        for h in range(2):
            scores = dot_nt(only_head(pair, h), key) + bias[...]
            peak = jnp.max(scores, axis=-1, keepdims=True)
            raised = jnp.exp(scores - peak)
            total = jnp.sum(raised, axis=-1, keepdims=True)
            halves.append(dot(raised.astype(bf16), value) / total)
            log_all = jnp.where(lane == 2 * j + h, peak + jnp.log(total), log_all)
        result[:, columns] = jnp.where(lane < 64, halves[0], halves[1])
    logs[...] = log_all


def head_rows(query, result, pull, length, width):
    lane = lax.broadcasted_iota(jnp.int32, (length, PAIR), 1)
    sums = jnp.zeros((length, PAIR), f32)
    for j in range(width // PAIR):
        columns = slice(j * PAIR, (j + 1) * PAIR)
        product = pull[:, columns].astype(f32) * result[:, columns]
        for h in range(2):
            total = jnp.sum(only_head(product, h), axis=-1, keepdims=True)
            sums = jnp.where(lane == 2 * j + h, total, sums)
    return sums.T


def mask_bias_turned(bias, place, query_labels, key_labels, length, causal):
    for s in range(4):
        holding = jnp.broadcast_to(key_labels[s], (length, length)).T
        same = holding == query_labels
        if causal:
            query = place * length + lax.broadcasted_iota(jnp.int32, (length, length), 1)
            key = (place ^ s) * length + lax.broadcasted_iota(jnp.int32, (length, length), 0)
            same = same & (key <= query)
        bias[s * length : (s + 1) * length] = jnp.where(same, 0.0, masked_score)


def attend_back(query, keys, values, bias, factor, result, logs, pull, dq, store):
    length, width = query.shape
    deltas = head_rows(query, result, pull, length, width)
    totals = logs[...].T
    for j in range(width // PAIR):
        columns = slice(j * PAIR, (j + 1) * PAIR)
        pair = query[:, columns] * jnp.asarray(factor, bf16)
        wanted = pull[:, columns]
        key, value = keys(j), values(j)
        key_turned = key.T
        dkey, dvalue, dquery = 0.0, 0.0, []
        for h in range(2):
            row = slice(2 * j + h, 2 * j + h + 1)
            asking, pulling = only_head(pair, h), only_head(wanted, h)
            chance = jnp.exp(dot_nt(key, asking) + bias[...] - totals[row])
            slope = (chance * (dot_nt(value, pulling) - deltas[row])).astype(bf16)
            dquery.append(dot(key_turned[h * 64 : h * 64 + 64], slope))
            dkey = dkey + dot(slope, asking)
            dvalue = dvalue + dot(chance.astype(bf16), pulling)
        dq[:, columns] = (jnp.concatenate(dquery, axis=0).T * factor).astype(bf16)
        store(j, dkey.astype(bf16), dvalue.astype(bf16))


def self_kernel(
    place, x0, x1, x2, x3, weight, query_bias, value_bias, out_weight, out_bias, gain, shift,
    ask_weight, ask_bias, pairs, query, result, logs, normed, scale, asked, bias, factor,
):
    length, width = query.shape
    blocks = (x0, x1, x2, x3)
    for s, block in enumerate(blocks):
        both = dot(block[:length], weight[:, width:])
        rows = slice(s * length, (s + 1) * length)
        pairs[rows, :width] = both[:, :width].astype(bf16)
        pairs[rows, width:] = (both[:, width:] + value_bias[...]).astype(bf16)
    query[...] = (dot(x0[:length], weight[:, :width]) + query_bias[...]).astype(bf16)
    labels = [block[length : length + 1, :length].astype(f32) for block in blocks]
    mask_bias(bias, place[0], labels[0], labels, length, True)
    attend(
        query,
        lambda j: pairs[:, j * PAIR : (j + 1) * PAIR],
        lambda j: pairs[:, width + j * PAIR : width + (j + 1) * PAIR],
        bias, factor, result, logs,
    )
    mixed = result[...].astype(bf16)
    before = x0[:length].astype(f32) + dot(mixed, out_weight[...]) + out_bias[...]
    first, normed[...], spread = norm_forward(before, gain[...], shift[...])
    scale[...] = jnp.broadcast_to(spread, scale.shape)
    asked[...] = (dot(first.astype(bf16), ask_weight[...]) + ask_bias[...]).astype(bf16)


def memory_views(blocks, length, width):
    def keys(j):
        return jnp.concatenate([m[:length, j * PAIR : (j + 1) * PAIR] for m in blocks], axis=0)

    def values(j):
        return jnp.concatenate(
            [m[:length, width + j * PAIR : width + (j + 1) * PAIR] for m in blocks], axis=0
        )

    return keys, values


def cross_kernel(
    number, asked, m0, m1, m2, m3, x0, normed1, gain1, shift1, out_weight, out_bias, gain2, shift2,
    grow, grow_bias, shrink, shrink_bias, gain3, shift3, cotangent,
    output, keep, away, small, delta, pull, result, logs,
    bias, sums, sem, factor, piece,
):
    length, width = asked.shape
    hidden = grow.shape[1]
    blocks = (m0, m1, m2, m3)
    asking = x0[length : length + 1, :length].astype(f32)
    labels = [m[length : length + 1, :length].astype(f32) for m in blocks]
    mask_bias(bias, None, asking, labels, length, False)
    keys, values = memory_views(blocks, length, width)
    attend(asked, keys, values, bias, factor, result, logs)
    crossed = result[...].astype(bf16)
    first = normed1[...] * gain1[...] + shift1[...]
    before = first + dot(crossed, out_weight[...]) + out_bias[...]
    second, normed2, scale2 = norm_forward(before, gain2[...], shift2[...])
    second_low = second.astype(bf16)
    inner = dot(second_low, grow[...]) + grow_bias[...]
    gate = 1.0 / (1.0 + jnp.exp(-inner))
    active = (inner * gate).astype(bf16)
    before = second + dot(active, shrink[...]) + shrink_bias[...]
    final, normed3, scale3 = norm_forward(before, gain3[...], shift3[...])
    output[...] = final.astype(bf16)

    incoming = cotangent[...].astype(f32)
    third, gain3_sum, shift3_sum = norm_backward(incoming, normed3, scale3, gain3[...])
    shrink_low = third.astype(bf16)
    sums[0:hidden] = dot_tn(active, shrink_low).astype(bf16)
    slope = gate * (1.0 + inner * (1.0 - gate))
    grow_low = (dot_nt(shrink_low, shrink[...]) * slope).astype(bf16)
    grown = dot_tn(second_low, grow_low).astype(bf16)
    for c in range(hidden // width):
        sums[hidden + c * width : hidden + (c + 1) * width] = grown[:, c * width : (c + 1) * width]
    second_gradient = third + dot_nt(grow_low, grow[...])
    cross_delta, gain2_sum, shift2_sum = norm_backward(
        second_gradient, normed2, scale2, gain2[...]
    )
    delta[...] = cross_delta
    cross_low = cross_delta.astype(bf16)
    sums[2 * hidden : 2 * hidden + width] = dot_tn(crossed, cross_low).astype(bf16)
    if sums.shape[0] > 2 * hidden + width:
        sums[2 * hidden + width :] = jnp.zeros_like(sums[2 * hidden + width :])
    copies = spread_pieces(number, sums, keep, away, piece, sem)
    pull[...] = dot_nt(cross_low, out_weight[...]).astype(bf16)
    grow_sum = column_total(grow_low)
    rows = [gain3_sum, shift3_sum, column_total(shrink_low), gain2_sum, shift2_sum,
            column_total(cross_low)]
    rows += [grow_sum[:, c * width : (c + 1) * width] for c in range(hidden // width)]
    rows += [jnp.zeros((SMALL_ROWS - len(rows), width), f32)]
    small[...] = jnp.concatenate(rows, axis=0)
    for copy in copies:
        copy.wait()


def spread_pieces(number, sums, keep, away, piece, sem):
    half = sums.shape[0] // piece // 2
    core, mine, other = number[0], number[1], number[2]
    copies = []
    for q in range(half):
        for t, (target, top, low) in enumerate(((keep, core, mine), (away, 1 - core, other))):
            start = pl.multiple_of(((q ^ low) + top * half) * piece, 16)
            copies.append(
                pltpu.make_async_copy(
                    sums.at[pl.ds(start, piece)],
                    target.at[pl.ds(q * piece, piece)],
                    sem.at[2 * q + t],
                )
            )
    for copy in copies:
        copy.start()
    return copies


def cross_back_kernel(
    asked, m0, m1, m2, m3, x0, pull, result, logs, near0, near1, far, asked_low, bias, factor
):
    length, width = asked.shape
    blocks = (m0, m1, m2, m3)
    asking = x0[length : length + 1, :length].astype(f32)
    labels = [m[length : length + 1, :length].astype(f32) for m in blocks]
    mask_bias_turned(bias, None, asking, labels, length, False)
    keys, values = memory_views(blocks, length, width)
    outs = ((near0, 0), (near1, 0), (far, 0), (far, 2 * length))

    def store(j, dkey, dvalue):
        for k, part in enumerate((dkey, dvalue)):
            for s, (out, row) in enumerate(outs):
                start = row + k * length
                out[start : start + length, j * PAIR : (j + 1) * PAIR] = part[
                    s * length : (s + 1) * length
                ]

    attend_back(asked, keys, values, bias, factor, result, logs, pull, asked_low, store)


def middle_kernel(
    asked_low, cross_delta, normed1, scale1, gain1, shift1, self_result, ask_weight,
    self_out_weight, small_in, late, delta, mixed_pull, small,
):
    width = asked_low.shape[1]
    normed = normed1[...]
    first_low = (normed * gain1[...] + shift1[...]).astype(bf16)
    first_gradient = cross_delta[...] + dot_nt(asked_low[...], ask_weight[...])
    self_delta, gain_sum, shift_sum = norm_backward(
        first_gradient, normed, scale1[:, 0:1], gain1[...]
    )
    delta[...] = self_delta
    self_low = self_delta.astype(bf16)
    mixed_pull[...] = dot_nt(self_low, self_out_weight[...]).astype(bf16)
    late[0:width] = dot_tn(first_low, asked_low[...]).astype(bf16)
    late[width : 2 * width] = dot_tn(self_result[...].astype(bf16), self_low).astype(bf16)
    small[...] = small_in[...]
    small[10:14] = jnp.concatenate(
        [column_total(asked_low[...]), gain_sum, shift_sum, column_total(self_low)], axis=0
    )


def self_back_kernel(
    place, query, pairs, x0, x1, x2, x3, pull, result, logs, dpairs, query_low, bias, factor
):
    length, width = query.shape
    blocks = (x0, x1, x2, x3)
    labels = [block[length : length + 1, :length].astype(f32) for block in blocks]
    mask_bias_turned(bias, place[0], labels[0], labels, length, True)

    def store(j, dkey, dvalue):
        dpairs[:, j * PAIR : (j + 1) * PAIR] = dkey
        dpairs[:, width + j * PAIR : width + (j + 1) * PAIR] = dvalue

    attend_back(
        query,
        lambda j: pairs[:, j * PAIR : (j + 1) * PAIR],
        lambda j: pairs[:, width + j * PAIR : width + (j + 1) * PAIR],
        bias, factor, result, logs, pull, query_low, store,
    )


def project_back_kernel(
    number, dpairs, query_low, x0, x1, x2, x3, delta, weight, late, small_in,
    keep, away, near0, near1, far, base, sums, last, sem, piece,
):
    length, width = query_low.shape
    blocks = (x0, x1, x2, x3)
    done = late.shape[0]
    sums[0:done] = late[...]
    sums[done : done + width] = dot_tn(x0[:length], query_low[...]).astype(bf16)
    for half in range(2):
        columns = slice(half * width, (half + 1) * width)
        total = jnp.zeros((width, width), f32)
        for s, block in enumerate(blocks):
            total = total + dot_tn(block[:length], dpairs[s * length : (s + 1) * length, columns])
        sums[done + (1 + half) * width : done + (2 + half) * width] = total.astype(bf16)
    if sums.shape[0] > done + 3 * width:
        sums[done + 3 * width :] = jnp.zeros_like(sums[done + 3 * width :])
    last[...] = small_in[...].astype(bf16)
    last[14:16] = jnp.concatenate(
        [column_total(query_low[...]), column_total(dpairs[:, width:])], axis=0
    ).astype(bf16)
    copies = spread_pieces(number, sums, keep, away, piece, sem)
    tail = pltpu.make_async_copy(
        last, away.at[pl.ds(keep.shape[0], SMALL_ROWS)], sem.at[len(copies)]
    )
    tail.start()
    outs = (near0.at[...], near1.at[...], far.at[0:length], far.at[length : 2 * length])
    for s in range(4):
        outs[s][...] = dot_nt(dpairs[s * length : (s + 1) * length], weight[:, width:]).astype(bf16)
    base[...] = delta[...] + dot_nt(query_low[...], weight[:, :width])
    for copy in copies:
        copy.wait()
    tail.wait()


def fold(keep, got, small, split, swap, after):
    count, width = keep.shape
    half = count // 2 if split else count
    extra = 0 if small is None else SMALL_ROWS
    args = [keep, got] + ([] if small is None else [small])
    outs = [jax.ShapeDtypeStruct((half, width), bf16)]
    separate = split or (swap and extra)
    if separate:
        outs.append(jax.ShapeDtypeStruct((half + extra, width), bf16))
    if extra:
        outs.append(jax.ShapeDtypeStruct((SMALL_ROWS, width), bf16))

    def kernel(*refs):
        mine, other = refs[0], refs[1]
        results = list(refs[len(args) :])
        kept = (mine[:half].astype(f32) + other[:half].astype(f32)).astype(bf16)
        results.pop(0)[...] = kept
        onward = results.pop(0) if separate else None
        if split:
            onward[:half] = (
                mine[half:count].astype(f32) + other[half:count].astype(f32)
            ).astype(bf16)
        elif separate:
            onward[:half] = kept
        if extra:
            total = (refs[2][...].astype(f32) + other[count:].astype(f32)).astype(bf16)
            results.pop(0)[...] = total
            if separate:
                onward[half:] = total

    res, token = call(kernel, outs, args, after=after, cost=30)
    res = list(res)
    kept = res.pop(0)
    onward = res.pop(0) if separate else (kept if swap else None)
    return kept, onward, (res.pop(0) if extra else None), token


def add_rows(parts, after, front=()):
    rows, width = parts[0][0].shape
    start = sum(a.shape[0] for a in front)
    args = [a for a, _ in parts] + list(front)

    def kernel(*refs):
        total = 0.0
        for (_, row), ref in zip(parts, refs, strict=False):
            total = total + ref[row : row + rows].astype(f32)
        place = 0
        for ref in refs[len(parts) : len(args)]:
            refs[-1][place : place + ref.shape[0]] = ref[...]
            place += ref.shape[0]
        refs[-1][start:] = total.astype(bf16)

    outs = [jax.ShapeDtypeStruct((start + rows, width), bf16)]
    (whole,), token = call(kernel, outs, args, after=after, cost=10)
    return whole, token


def join(parts, after):
    count = sum(part.shape[0] for part in parts)

    def kernel(*refs):
        position = 0
        for part in refs[: len(parts)]:
            refs[-1][position : position + part.shape[0]] = part[...]
            position += part.shape[0]

    outs = [jax.ShapeDtypeStruct((count, parts[0].shape[1]), bf16)]
    (whole,), token = call(kernel, outs, list(parts), after=after, cost=30)
    return whole, token


ORDER = "ELELLELELmxELLi"


class Chain:
    def __init__(self, keep, away, small, rows, seq):
        self.rows, self.seq = rows, seq
        self.core = [(r * seq + z, (r ^ 1) * seq + z) for r in range(rows) for z in range(seq)]
        self.keep, self.small = keep, small
        self.got = send(away, self.core)
        self.steps = len(bit_orders(rows)[0])
        self.k = 0
        self.mark = None
        self.mine = self.other = None

    def step(self, after=()):
        k, n = self.k, self.steps
        self.k += 1
        if k <= n:
            self.keep, onward, self.small, self.mark = fold(
                self.keep, self.got, self.small, k < n - 1, k == n - 1, after
            )
            if k < n:
                self.got = send(onward, step_route(self.rows, self.seq, k))
            else:
                self.mine, self.other = [self.keep], [send(self.keep, self.core)]
                self.got = send(self.keep, step_route(self.rows, self.seq, n - 2))
        else:
            back = 2 * n - 2 - k
            if back < 0:
                self.got, _ = lax.optimization_barrier((self.got, after))
            self.mine.append(self.got)
            self.other.append(send(self.got, self.core))
            if back >= 0:
                whole, self.mark = join(self.mine, after)
                self.got = send(whole, step_route(self.rows, self.seq, back))

    @property
    def count(self):
        return 2 * self.steps


def place_parts(number, groups, scratch, sems, piece, half):
    core = number[0]
    waits = []
    for group, (top, low) in enumerate(((core, number[1]), (1 - core, number[2]))):
        position = 0
        for i, part in enumerate(groups[group]):
            sem = sems.at[group * len(groups[0]) + i]
            for t in range(part.shape[0] // piece):
                start = pl.multiple_of((((position + t) ^ low) + top * half) * piece, 16)
                pltpu.make_async_copy(
                    part.at[pl.ds(t * piece, piece)], scratch.at[pl.ds(start, piece)], sem
                ).start()
            position += part.shape[0] // piece
            waits.append(pltpu.make_async_copy(part, scratch.at[pl.ds(0, part.shape[0])], sem))
    return waits


def finish_kernel(number, *refs, parts, piece, half, layout, moves, smalls):
    groups = (refs[:parts], refs[parts : 2 * parts])
    refs = list(refs[2 * parts :])
    if smalls:
        small, small_far = refs.pop(0), refs.pop(0)
    home = refs.pop(0)
    sums, refs = refs[: len(layout)], refs[len(layout) :]
    small_out, refs = refs[: len(smalls)], refs[len(smalls) :]
    move_out, refs = refs[: len(moves)], refs[len(moves) :]
    token, scratch, wide, between, both, sems, out_sems = refs
    waits = place_parts(number, groups, scratch, sems, piece, half)
    moving = pltpu.make_async_copy(home, between, sems.at[2 * parts])
    moving.start()
    copies = []

    def out(source, target):
        copies.append(pltpu.make_async_copy(source, target, out_sems.at[len(copies)]))
        copies[-1].start()

    if smalls:
        both[...] = 0.5 * (small[...].astype(f32) + small_far[...].astype(f32))
        for (first, count), target in zip(smalls, small_out, strict=True):
            for i in range(count):
                width = both.shape[1]
                out(both.at[pl.ds(first + i, 1)], target.at[:, pl.ds(i * width, width)])
    moving.wait()
    for pieces, target in zip(moves, move_out, strict=True):
        for row, count, column in pieces:
            out(between.at[pl.ds(row, count)], target.at[:, pl.ds(column, between.shape[1])])
    for wait in waits:
        wait.wait()
    row = 0
    for target, blocks in zip(sums, layout, strict=True):
        for to_row, to_column, count in blocks:
            width = scratch.shape[1]
            wide[row : row + count] = scratch[row : row + count].astype(f32)
            out(
                wide.at[pl.ds(row, count)],
                target.at[pl.ds(to_row, count), pl.ds(to_column, width)],
            )
            row = row + count
    token[...] = jnp.zeros_like(token)
    for copy in copies:
        copy.wait()


def finish(number, chain, piece, half, shapes, layout, home, moves, small_far=None, smalls=(), after=()):
    parts = len(chain.mine)
    width = chain.mine[0].shape[1]
    total = 2 * half * piece
    hbm = pl.BlockSpec(memory_space=pltpu.HBM)
    vmem = pl.BlockSpec(memory_space=pltpu.VMEM)
    extra = [chain.small, small_far] if smalls else []
    count = sum(len(b) for b in layout) + sum(len(m) for m in moves) + sum(n for _, n in smalls)
    moved = [jax.ShapeDtypeStruct((m[0][1], len(m) * width), bf16) for m in moves]

    def kernel(*refs):
        given = 1 + 2 * parts + len(extra) + 1
        finish_kernel(
            *refs[:given], *refs[given + len(after) :],
            parts=parts, piece=piece, half=half, layout=layout, moves=moves, smalls=smalls,
        )

    res = pl.pallas_call(
        kernel,
        in_specs=[pl.BlockSpec(memory_space=pltpu.SMEM)] + [hbm] * (2 * parts)
        + [vmem] * len(extra) + [hbm] + [vmem] * len(after),
        out_specs=[hbm] * (len(shapes) + len(smalls) + len(moves)) + [vmem],
        out_shape=[jax.ShapeDtypeStruct(s, f32) for s in shapes]
        + [jax.ShapeDtypeStruct((1, n * width), f32) for _, n in smalls]
        + moved + [TOKEN],
        scratch_shapes=[
            pltpu.VMEM((total, width), bf16),
            pltpu.VMEM((total, width), f32),
            pltpu.VMEM(home.shape, bf16),
            pltpu.VMEM((SMALL_ROWS, width), f32),
            pltpu.SemaphoreType.DMA((2 * parts + 1,)),
            pltpu.SemaphoreType.DMA((count,)),
        ],
        compiler_params=pltpu.CompilerParams(vmem_limit_bytes=20 * 1024 * 1024),
        cost_estimate=taking(6),
    )(number, *chain.mine, *chain.other, *extra, home, *after)
    return res[:-1], res[-1]


def pack_kernel(inputs, memory, target, source, x, m):
    length = inputs.shape[0]
    for value, labels, out in ((inputs, target, x), (memory, source, m)):
        out[:length] = value[...]
        out[length:] = jnp.zeros_like(out[length:])
        out[length : length + 1, :length] = labels[...].astype(f32).astype(bf16)


def pack(inputs, memory, target, source):
    length = inputs.shape[0]
    outs = [jax.ShapeDtypeStruct((length + 16, a.shape[1]), bf16) for a in (inputs, memory)]
    return call(pack_kernel, outs, [inputs, memory, target, source], cost=2)[0]


def piece_rows(count, pieces):
    return -(-count // (pieces * 16)) * 16


def shards(
    inputs, memory, target_segments, memory_segments, self_project, self_query_bias,
    self_value_bias, self_output, self_output_bias, self_norm_gain, self_norm_bias, cross_query,
    cross_query_bias, cross_output, cross_output_bias, cross_norm_gain, cross_norm_bias,
    expand_weight, expand_bias, contract_weight, contract_bias, final_norm_gain, final_norm_bias,
    cotangent,
):
    rows, seq = lax.axis_size("rows"), lax.axis_size("seq")
    r, z = lax.axis_index("rows"), lax.axis_index("seq")
    _, length, width = inputs.shape
    hidden = expand_weight.shape[1]
    factor = float(width // HEADS) ** (-0.5)
    home = home_route(rows, seq)
    core = [(a * seq + b, (a ^ 1) * seq + b) for a in range(rows) for b in range(seq)]
    side = [(a * seq + b, a * seq + (b ^ 1)) for a in range(rows) for b in range(seq)]
    orders = bit_orders(rows)
    half = 2 ** (len(orders[0]) - 1)
    lows = [low_number(rows, order[:-1], r, z) for order in orders]
    is_one = (r & 1) == 1
    place = (z & 1) + 2 * (r & 1)
    number = jnp.stack([
        r & 1, jnp.where(is_one, lows[1], lows[0]), jnp.where(is_one, lows[0], lows[1]), place,
    ]).astype(jnp.int32)

    def line(vector):
        return vector.reshape(1, -1)

    packed_inputs, packed_memory = pack(inputs[0], memory[0], target_segments, memory_segments)
    x0 = send(packed_inputs, home)
    m0 = send(packed_memory, home)
    x1 = send(x0, side)
    x2 = send(x0, core)
    m1 = send(m0, side)
    m2 = send(m0, core)
    x3 = send(x1, core)
    m3 = send(m1, core)
    cotangent, _ = lax.optimization_barrier((cotangent, x0))
    pulled = send(cotangent[0], home)

    def shape(*dims, dtype=f32):
        return jax.ShapeDtypeStruct(dims, dtype)

    def low(*dims):
        return jax.ShapeDtypeStruct(dims, bf16)

    vmem = pl.BlockSpec(memory_space=pltpu.VMEM)
    any_space = pl.BlockSpec(memory_space=pl.ANY)
    bias_space = pltpu.VMEM((length, 4 * length), f32)
    bias_turned = pltpu.VMEM((4 * length, length), f32)

    (pairs, query, self_result, self_logs, normed1, scale1, asked), _ = call(
        functools.partial(self_kernel, factor=factor),
        [
            low(4 * length, 2 * width), low(length, width), shape(length, width),
            shape(length, PAIR), shape(length, width), shape(length, PAIR), low(length, width),
        ],
        [
            number[3:4], x0, x1, x2, x3, self_project, line(self_query_bias),
            line(self_value_bias), self_output, line(self_output_bias), line(self_norm_gain),
            line(self_norm_bias), cross_query, line(cross_query_bias),
        ],
        scratch=[bias_space],
        lazy=range(1, 14),
        cost=9,
        limit=60,
    )

    early_piece = piece_rows(2 * hidden + width, 2 * half)
    (output, early_keep, early_away, small, cross_delta, crossed_pull, cross_result, cross_logs), _ = call(
        functools.partial(cross_kernel, factor=factor, piece=early_piece),
        [
            low(length, width), low(half * early_piece, width), low(half * early_piece, width),
            shape(SMALL_ROWS, width), shape(length, width), low(length, width),
            shape(length, width), shape(length, PAIR),
        ],
        [
            number, asked, m0, m1, m2, m3, x0, normed1, line(self_norm_gain),
            line(self_norm_bias), cross_output, line(cross_output_bias), line(cross_norm_gain),
            line(cross_norm_bias), expand_weight, line(expand_bias), contract_weight,
            line(contract_bias), line(final_norm_gain), line(final_norm_bias), pulled,
        ],
        scratch=[
            bias_space,
            pltpu.VMEM((2 * half * early_piece, width), bf16),
            pltpu.SemaphoreType.DMA((2 * half,)),
        ],
        lazy=[2, 3, 4, 5, 6, *range(8, 21)],
        out_specs=[vmem, any_space, any_space] + [vmem] * 5,
        cost=15,
        limit=44,
    )
    early = Chain(early_keep, early_away, None, rows, seq)

    (mem_near0, mem_near1, mem_far, asked_low), token = call(
        functools.partial(cross_back_kernel, factor=factor),
        [low(2 * length, width), low(2 * length, width), low(4 * length, width),
         low(length, width)],
        [asked, m0, m1, m2, m3, x0, crossed_pull, cross_result, cross_logs],
        scratch=[bias_turned],
        lazy=range(1, 6),
        cost=8,
    )
    early.step((token,))
    mem_far = send(mem_far, core)

    (late, self_delta, mixed_pull, small), token = call(
        middle_kernel,
        [low(2 * width, width), shape(length, width), low(length, width),
         shape(SMALL_ROWS, width)],
        [
            asked_low, cross_delta, normed1, scale1, line(self_norm_gain), line(self_norm_bias),
            self_result, cross_query, self_output, small,
        ],
        lazy=[4, 5, 7, 8],
        cost=3,
        after=(early.mark,),
    )
    onward, token = add_rows([(mem_near1, 0), (mem_far, 2 * length)], (token,))
    mem_got = send(onward, side)

    (dpairs, query_low), token = call(
        functools.partial(self_back_kernel, factor=factor),
        [low(4 * length, 2 * width), low(length, width)],
        [number[3:4], query, pairs, x0, x1, x2, x3, mixed_pull, self_result, self_logs],
        scratch=[bias_turned],
        lazy=range(3, 7),
        cost=8,
        after=(token,),
    )
    early.step((token,))

    late_piece = piece_rows(5 * width, 2 * half)
    (late_keep, late_away, in_near0, in_near1, in_far, base), token = call(
        functools.partial(project_back_kernel, piece=late_piece),
        [
            low(half * late_piece, width), low(half * late_piece + SMALL_ROWS, width),
            low(length, width), low(length, width), low(2 * length, width), shape(length, width),
        ],
        [number, dpairs, query_low, x0, x1, x2, x3, self_delta, self_project, late, small],
        scratch=[
            pltpu.VMEM((2 * half * late_piece, width), bf16),
            pltpu.VMEM((SMALL_ROWS, width), bf16),
            pltpu.SemaphoreType.DMA((2 * half + 1,)),
        ],
        lazy=[3, 4, 5, 6, 8],
        out_specs=[any_space, any_space] + [vmem] * 4,
        cost=5,
        after=(early.mark,),
    )
    late = Chain(late_keep, late_away, late_away[-SMALL_ROWS:], rows, seq)
    in_far = send(in_far, core)
    for name in ORDER:
        if name in "EL":
            chain = early if name == "E" else late
            chain.step((token,))
            token = chain.mark
        elif name == "m":
            early_home, token = add_rows(
                [(mem_near0, 0), (mem_far, 0), (mem_got, 0)], (token,), (output,)
            )
            early_home = send(early_home, home)
        elif name == "x":
            onward, token = add_rows([(in_near1, 0), (in_far, length)], (token,))
            in_got = send(onward, side)
        elif name == "i":
            late_home, token = add_rows(
                [(base, 0), (in_near0, 0), (in_far, 0), (in_got, 0)], (token,)
            )
            late_home = send(late_home, home)
    early.step((token,))
    small_far = send(late.small, core)

    blocks = range(hidden // width)
    (gradient_contract, gradient_expand, gradient_cross_output, output, memory_gradient), token = (
        finish(
            number, early, early_piece, half,
            [(hidden, width), (width, hidden), (width, width)],
            [[(c * width, 0, width) for c in blocks], [(0, c * width, width) for c in blocks],
             [(0, 0, width)]],
            early_home,
            [[(0, length, 0)], [(length, length, 0), (2 * length, length, width)]],
        )
    )
    late.step((token,))
    smalls = [(0, 1), (1, 1), (2, 1), (3, 1), (4, 1), (5, 1), (6, hidden // width)]
    smalls += [(i, 1) for i in range(10, 16)]
    (
        gradient_cross_query, gradient_self_output, gradient_self_project, gradient_final_gain,
        gradient_final_bias, gradient_contract_bias, gradient_cross_gain, gradient_cross_bias,
        gradient_cross_output_bias, gradient_expand_bias, gradient_cross_query_bias,
        gradient_self_gain, gradient_self_bias, gradient_self_output_bias, gradient_query_bias,
        gradient_value_bias, input_gradient,
    ), _ = finish(
        number, late, late_piece, half,
        [(width, width), (width, width), (width, 3 * width)],
        [[(0, 0, width)], [(0, 0, width)], [(0, c * width, width) for c in range(3)]],
        late_home,
        [[(0, length, 0)]],
        small_far=small_far,
        smalls=smalls,
        after=(token,),
    )

    return (
        output[None],
        input_gradient[None],
        memory_gradient[None],
        gradient_self_project,
        gradient_query_bias.reshape(-1),
        gradient_value_bias.reshape(-1),
        gradient_self_output,
        gradient_self_output_bias.reshape(-1),
        gradient_self_gain.reshape(-1),
        gradient_self_bias.reshape(-1),
        gradient_cross_query,
        gradient_cross_query_bias.reshape(-1),
        gradient_cross_output,
        gradient_cross_output_bias.reshape(-1),
        gradient_cross_gain.reshape(-1),
        gradient_cross_bias.reshape(-1),
        gradient_expand,
        gradient_expand_bias.reshape(-1),
        gradient_contract,
        gradient_contract_bias.reshape(-1),
        gradient_final_gain.reshape(-1),
        gradient_final_bias.reshape(-1),
    )


def solution(mesh):
    tokens = P("rows", "seq", None)
    in_specs = (tokens, tokens, P("rows", "seq"), P("rows", "seq")) + (P(),) * 19 + (tokens,)
    out_specs = (tokens,) * 3 + (P(),) * 19
    return jax.shard_map(shards, mesh=mesh, in_specs=in_specs, out_specs=out_specs, check_vma=False)
```

```python
import functools

import jax
import jax.numpy as jnp
from jax import lax
from jax.experimental import pallas as pl
from jax.experimental.pallas import tpu as pltpu
from jax.sharding import PartitionSpec as P

HEADS = 8
PAIR = 128
SMALL_ROWS = 16
masked_score = -1e30
epsilon = 1e-05
f32 = jnp.float32
bf16 = jnp.bfloat16
BOTH = ("rows", "seq")


def dot(left, right):
    return jnp.dot(left, right, preferred_element_type=f32)


def dot_nt(left, right):
    return lax.dot_general(left, right, (((1,), (1,)), ((), ())), preferred_element_type=f32)


def dot_tn(left, right):
    return lax.dot_general(left, right, (((0,), (0,)), ((), ())), preferred_element_type=f32)


def norm_forward(value, gain, shift):
    center = jnp.mean(value, axis=-1, keepdims=True)
    centred = value - center
    scale = lax.rsqrt(jnp.mean(centred * centred, axis=-1, keepdims=True) + epsilon)
    normed = centred * scale
    return normed * gain + shift, normed, scale


def norm_backward(incoming, normed, scale, gain):
    weighted = incoming * gain
    spread = weighted - jnp.mean(weighted, axis=-1, keepdims=True)
    spread = spread - normed * jnp.mean(weighted * normed, axis=-1, keepdims=True)
    return scale * spread, column_total(incoming * normed), column_total(incoming)


def column_total(value):
    return jnp.sum(value.astype(f32), axis=0, keepdims=True)


def head_lanes(shape, h):
    lane = lax.broadcasted_iota(jnp.int32, shape, 1)
    return (lane < 64) if h == 0 else (lane >= 64)


def only_head(value, h):
    return jnp.where(head_lanes(value.shape, h), value, jnp.zeros_like(value))


def flat_pairs(rows, seq, partner):
    return [(r * seq + z, partner(r, z)) for r in range(rows) for z in range(seq)]


def home_route(rows, seq):
    def partner(r, z):
        if (r & 1) == z // 2:
            return r * seq + z
        return (r ^ 1) * seq + (z ^ 2)

    return flat_pairs(rows, seq, partner)


def bit_orders(rows):
    count = rows.bit_length() - 2
    bits = [("r", 1 << (k + 1)) for k in range(count)]
    tail = [("z", 1), ("z", 2)]
    return bits + tail, bits[::-1] + tail


def step_route(rows, seq, k):
    orders = bit_orders(rows)

    def partner(r, z):
        kind, mask = orders[r & 1][k]
        return (r ^ mask) * seq + z if kind == "r" else r * seq + (z ^ mask)

    return flat_pairs(rows, seq, partner)


def low_number(rows, order, r, z):
    number = jnp.int32(0)
    for kind, mask in order:
        bit = jnp.where(((r if kind == "r" else z) & mask) != 0, 1, 0)
        number = number * 2 + bit
    return number


def send(value, route):
    return lax.ppermute(value, BOTH, route)


def taking(us):
    return pl.CostEstimate(
        flops=int(us * 1.15e9), bytes_accessed=int(us * 3.6e6), transcendentals=0
    )


class Lazy:
    def __init__(self, far, near, sem):
        self.copy, self.near, self.waiting = pltpu.make_async_copy(far, near, sem), near, True
        self.copy.start()

    @property
    def shape(self):
        return self.near.shape

    def __getitem__(self, index):
        if self.waiting:
            self.copy.wait()
            self.waiting = False
        return self.near[index]


TOKEN = jax.ShapeDtypeStruct((8, 128), f32)


def call(kernel, outs, args, scratch=(), lazy=(), out_specs=None, cost=None, after=(), present=(),
         limit=24):
    vmem = pl.BlockSpec(memory_space=pltpu.VMEM)
    smem = pl.BlockSpec(memory_space=pltpu.SMEM)
    hbm = pl.BlockSpec(memory_space=pltpu.HBM)
    count = len(args)
    lazy = list(lazy)

    def spec(i, arg):
        if i in lazy:
            return hbm
        return smem if arg.dtype == jnp.int32 and arg.ndim == 1 else vmem

    def inner(*refs):
        given = list(refs[:count])
        rest = refs[count + len(after) + len(present) :]
        results, token, held = rest[: len(outs)], rest[len(outs)], rest[len(outs) + 1 :]
        near, held = held[: len(lazy)], held[len(lazy) :]
        if lazy:
            sems, held = held[0], held[1:]
            for k, i in enumerate(lazy):
                given[i] = Lazy(given[i], near[k], sems.at[k])
        kernel(*given, *results, *held)
        for i in lazy:
            if given[i].waiting:
                given[i].copy.wait()
        token[...] = jnp.zeros_like(token)

    spaces = [pltpu.VMEM(args[i].shape, args[i].dtype) for i in lazy]
    if lazy:
        spaces.append(pltpu.SemaphoreType.DMA((len(lazy),)))
    res = pl.pallas_call(
        inner,
        out_shape=list(outs) + [TOKEN],
        in_specs=[spec(i, a) for i, a in enumerate(args)]
        + [vmem] * len(after) + [hbm] * len(present),
        out_specs=(out_specs if out_specs is not None else [vmem] * len(outs)) + [vmem],
        scratch_shapes=spaces + list(scratch),
        compiler_params=pltpu.CompilerParams(vmem_limit_bytes=limit * 1024 * 1024),
        cost_estimate=None if cost is None else taking(cost),
    )(*args, *after, *present)
    return res[:-1], res[-1]


def mask_bias(bias, place, query_labels, key_labels, length, causal):
    asking = jnp.broadcast_to(query_labels, (length, length)).T
    for s in range(4):
        same = asking == key_labels[s]
        if causal:
            query = place * length + lax.broadcasted_iota(jnp.int32, (length, length), 0)
            key = (place ^ s) * length + lax.broadcasted_iota(jnp.int32, (length, length), 1)
            same = same & (key <= query)
        bias[:, s * length : (s + 1) * length] = jnp.where(same, 0.0, masked_score)


def attend(query, keys, values, bias, factor, result, logs):
    length, width = query.shape
    lane = lax.broadcasted_iota(jnp.int32, (length, PAIR), 1)
    log_all = jnp.zeros((length, PAIR), f32)
    for j in range(width // PAIR):
        columns = slice(j * PAIR, (j + 1) * PAIR)
        pair = query[:, columns] * jnp.asarray(factor, bf16)
        key, value = keys(j), values(j)
        halves = []
        for h in range(2):
            scores = dot_nt(only_head(pair, h), key) + bias[...]
            peak = jnp.max(scores, axis=-1, keepdims=True)
            raised = jnp.exp(scores - peak)
            total = jnp.sum(raised, axis=-1, keepdims=True)
            halves.append(dot(raised.astype(bf16), value) / total)
            log_all = jnp.where(lane == 2 * j + h, peak + jnp.log(total), log_all)
        result[:, columns] = jnp.where(lane < 64, halves[0], halves[1])
    logs[...] = log_all


def head_rows(query, result, pull, length, width):
    lane = lax.broadcasted_iota(jnp.int32, (length, PAIR), 1)
    sums = jnp.zeros((length, PAIR), f32)
    for j in range(width // PAIR):
        columns = slice(j * PAIR, (j + 1) * PAIR)
        product = pull[:, columns].astype(f32) * result[:, columns]
        for h in range(2):
            total = jnp.sum(only_head(product, h), axis=-1, keepdims=True)
            sums = jnp.where(lane == 2 * j + h, total, sums)
    return sums.T


def mask_bias_turned(bias, place, query_labels, key_labels, length, causal):
    for s in range(4):
        holding = jnp.broadcast_to(key_labels[s], (length, length)).T
        same = holding == query_labels
        if causal:
            query = place * length + lax.broadcasted_iota(jnp.int32, (length, length), 1)
            key = (place ^ s) * length + lax.broadcasted_iota(jnp.int32, (length, length), 0)
            same = same & (key <= query)
        bias[s * length : (s + 1) * length] = jnp.where(same, 0.0, masked_score)


def attend_back(query, keys, values, bias, factor, result, logs, pull, dq, store):
    length, width = query.shape
    deltas = head_rows(query, result, pull, length, width)
    totals = logs[...].T
    for j in range(width // PAIR):
        columns = slice(j * PAIR, (j + 1) * PAIR)
        pair = query[:, columns] * jnp.asarray(factor, bf16)
        wanted = pull[:, columns]
        key, value = keys(j), values(j)
        key_turned = key.T
        dkey, dvalue, dquery = 0.0, 0.0, []
        for h in range(2):
            row = slice(2 * j + h, 2 * j + h + 1)
            asking, pulling = only_head(pair, h), only_head(wanted, h)
            chance = jnp.exp(dot_nt(key, asking) + bias[...] - totals[row])
            slope = (chance * (dot_nt(value, pulling) - deltas[row])).astype(bf16)
            dquery.append(dot(key_turned[h * 64 : h * 64 + 64], slope))
            dkey = dkey + dot(slope, asking)
            dvalue = dvalue + dot(chance.astype(bf16), pulling)
        dq[:, columns] = (jnp.concatenate(dquery, axis=0).T * factor).astype(bf16)
        store(j, dkey.astype(bf16), dvalue.astype(bf16))


def rows_of(vectors, first, count):
    return [vectors[i : i + 1] for i in range(first, first + count)]


def row_labels(marks, row, length):
    return [marks[row : row + 1, s * length : (s + 1) * length] for s in range(4)]


def self_kernel(
    place, x0, x1, x2, x3, weight, out_weight, ask_weight, vectors,
    pairs, query, result, logs, normed, scale, asked, marks, bias, factor,
):
    length, width = query.shape
    blocks = (x0, x1, x2, x3)
    query_bias, value_bias, out_bias, gain, shift, ask_bias = rows_of(vectors, 0, 6)
    for s, block in enumerate(blocks):
        both = dot(block[:length], weight[:, width:])
        rows = slice(s * length, (s + 1) * length)
        pairs[rows, :width] = both[:, :width].astype(bf16)
        pairs[rows, width:] = (both[:, width:] + value_bias).astype(bf16)
    query[...] = (dot(x0[:length], weight[:, :width]) + query_bias).astype(bf16)
    for s, block in enumerate(blocks):
        columns = slice(s * length, (s + 1) * length)
        marks[:, columns] = block[length : length + 8, :length].astype(f32)
    labels = row_labels(marks, 0, length)
    mask_bias(bias, place[0], labels[0], labels, length, True)
    attend(
        query,
        lambda j: pairs[:, j * PAIR : (j + 1) * PAIR],
        lambda j: pairs[:, width + j * PAIR : width + (j + 1) * PAIR],
        bias, factor, result, logs,
    )
    mixed = result[...].astype(bf16)
    before = x0[:length].astype(f32) + dot(mixed, out_weight[...]) + out_bias
    first, normed[...], spread = norm_forward(before, gain, shift)
    scale[...] = jnp.broadcast_to(spread, scale.shape)
    asked[...] = (dot(first.astype(bf16), ask_weight[...]) + ask_bias).astype(bf16)


def memory_views(blocks, length, width):
    def keys(j):
        return jnp.concatenate([m[:length, j * PAIR : (j + 1) * PAIR] for m in blocks], axis=0)

    def values(j):
        return jnp.concatenate(
            [m[:length, width + j * PAIR : width + (j + 1) * PAIR] for m in blocks], axis=0
        )

    return keys, values


def cross_kernel(
    number, asked, m0, m1, m2, m3, marks, normed1, out_weight, grow, shrink, vectors, cotangent,
    output, keep_a, away_a, keep_b, away_b, small, delta, pull, result, logs,
    bias, sums_a, sums_b, factor, piece_a, piece_b,
):
    length, width = asked.shape
    hidden = grow.shape[1]
    blocks = (m0, m1, m2, m3)
    gain1, shift1 = rows_of(vectors, 3, 2)
    out_bias, gain2, shift2, shrink_bias, gain3, shift3 = rows_of(vectors, 6, 6)
    grow_bias = jnp.concatenate(rows_of(vectors, 12, hidden // width), axis=1)
    asking, labels = row_labels(marks, 0, length)[0], row_labels(marks, 1, length)
    mask_bias(bias, None, asking, labels, length, False)
    keys, values = memory_views(blocks, length, width)
    attend(asked, keys, values, bias, factor, result, logs)
    crossed = result[...].astype(bf16)
    first = normed1[...] * gain1 + shift1
    before = first + dot(crossed, out_weight[...]) + out_bias
    second, normed2, scale2 = norm_forward(before, gain2, shift2)
    second_low = second.astype(bf16)
    inner = dot(second_low, grow[...]) + grow_bias
    gate = 1.0 / (1.0 + jnp.exp(-inner))
    active = (inner * gate).astype(bf16)
    before = second + dot(active, shrink[...]) + shrink_bias
    final, normed3, scale3 = norm_forward(before, gain3, shift3)
    output[...] = final.astype(bf16)

    incoming = cotangent[...].astype(f32)
    third, gain3_sum, shift3_sum = norm_backward(incoming, normed3, scale3, gain3)
    shrink_low = third.astype(bf16)
    sums_a[0:hidden] = dot_tn(active, shrink_low).astype(bf16)
    fill_up(sums_a, hidden)
    slope = gate * (1.0 + inner * (1.0 - gate))
    grow_low = (dot_nt(shrink_low, shrink[...]) * slope).astype(bf16)
    grown = dot_tn(second_low, grow_low).astype(bf16)
    for c in range(hidden // width):
        sums_b[c * width : (c + 1) * width] = grown[:, c * width : (c + 1) * width]
    second_gradient = third + dot_nt(grow_low, grow[...])
    cross_delta, gain2_sum, shift2_sum = norm_backward(
        second_gradient, normed2, scale2, gain2
    )
    delta[...] = cross_delta
    cross_low = cross_delta.astype(bf16)
    sums_b[hidden : hidden + width] = dot_tn(crossed, cross_low).astype(bf16)
    fill_up(sums_b, hidden + width)
    spread_pieces(number, sums_a, keep_a, away_a, piece_a)
    spread_pieces(number, sums_b, keep_b, away_b, piece_b)
    pull[...] = dot_nt(cross_low, out_weight[...]).astype(bf16)
    grow_sum = column_total(grow_low)
    rows = [gain3_sum, shift3_sum, column_total(shrink_low), gain2_sum, shift2_sum,
            column_total(cross_low)]
    rows += [grow_sum[:, c * width : (c + 1) * width] for c in range(hidden // width)]
    rows += [jnp.zeros((SMALL_ROWS - len(rows), width), f32)]
    small[...] = jnp.concatenate(rows, axis=0)


def fill_up(sums, count):
    if sums.shape[0] > count:
        sums[count:] = jnp.zeros_like(sums[count:])


def spread_pieces(number, sums, keep, away, piece):
    half = sums.shape[0] // piece // 2
    core, mine, other = number[0], number[1], number[2]
    for q in range(half):
        for target, top, low in ((keep, core, mine), (away, 1 - core, other)):
            start = pl.multiple_of(((q ^ low) + top * half) * piece, 16)
            target[q * piece : (q + 1) * piece] = sums[pl.ds(start, piece)]


def cross_back_kernel(
    asked, m0, m1, m2, m3, marks, pull, result, logs, near0, near1, far, asked_low, bias, factor
):
    length, width = asked.shape
    blocks = (m0, m1, m2, m3)
    asking, labels = row_labels(marks, 0, length)[0], row_labels(marks, 1, length)
    mask_bias_turned(bias, None, asking, labels, length, False)
    keys, values = memory_views(blocks, length, width)
    outs = ((near0, 0), (near1, 0), (far, 0), (far, 2 * length))

    def store(j, dkey, dvalue):
        for k, part in enumerate((dkey, dvalue)):
            for s, (out, row) in enumerate(outs):
                start = row + k * length
                out[start : start + length, j * PAIR : (j + 1) * PAIR] = part[
                    s * length : (s + 1) * length
                ]

    attend_back(asked, keys, values, bias, factor, result, logs, pull, asked_low, store)


def middle_kernel(
    asked_low, cross_delta, normed1, scale1, vectors, self_result, ask_weight,
    self_out_weight, small_in, late, delta, mixed_pull, small,
):
    width = asked_low.shape[1]
    gain1, shift1 = rows_of(vectors, 3, 2)
    normed = normed1[...]
    first_low = (normed * gain1 + shift1).astype(bf16)
    first_gradient = cross_delta[...] + dot_nt(asked_low[...], ask_weight[...])
    self_delta, gain_sum, shift_sum = norm_backward(
        first_gradient, normed, scale1[:, 0:1], gain1
    )
    delta[...] = self_delta
    self_low = self_delta.astype(bf16)
    mixed_pull[...] = dot_nt(self_low, self_out_weight[...]).astype(bf16)
    late[0:width] = dot_tn(first_low, asked_low[...]).astype(bf16)
    late[width : 2 * width] = dot_tn(self_result[...].astype(bf16), self_low).astype(bf16)
    small[...] = small_in[...]
    small[10:14] = jnp.concatenate(
        [column_total(asked_low[...]), gain_sum, shift_sum, column_total(self_low)], axis=0
    )


def self_back_kernel(
    place, query, pairs, marks, pull, result, logs, dpairs, query_low, bias, factor
):
    length, width = query.shape
    labels = row_labels(marks, 0, length)
    mask_bias_turned(bias, place[0], labels[0], labels, length, True)

    def store(j, dkey, dvalue):
        dpairs[:, j * PAIR : (j + 1) * PAIR] = dkey
        dpairs[:, width + j * PAIR : width + (j + 1) * PAIR] = dvalue

    attend_back(
        query,
        lambda j: pairs[:, j * PAIR : (j + 1) * PAIR],
        lambda j: pairs[:, width + j * PAIR : width + (j + 1) * PAIR],
        bias, factor, result, logs, pull, query_low, store,
    )


def project_sums_kernel(
    number, dpairs, query_low, x0, x1, x2, x3, late, small_in,
    keep, away, sums, turned, piece,
):
    length, width = query_low.shape
    done = late.shape[0]
    sums[0:done] = late[...]
    for s, block in enumerate((x0, x1, x2, x3)):
        turned[:, s * length : (s + 1) * length] = block[:length].T
    sums[done : done + width] = dot(turned[:, :length], query_low[...]).astype(bf16)
    for half in range(2):
        total = dot(turned[...], dpairs[:, half * width : (half + 1) * width])
        sums[done + (1 + half) * width : done + (2 + half) * width] = total.astype(bf16)
    fill_up(sums, done + 3 * width)
    spread_pieces(number, sums, keep, away, piece)
    rows = keep.shape[0]
    sums_small = [column_total(query_low[...]), column_total(dpairs[:, width:])]
    whole = jnp.concatenate([small_in[:14]] + sums_small, axis=0)
    away[rows : rows + SMALL_ROWS] = whole.astype(bf16)


def project_back_kernel(dpairs, query_low, delta, weight, near0, near1, far, base):
    length, width = query_low.shape
    outs = (near0.at[...], near1.at[...], far.at[0:length], far.at[length : 2 * length])
    for s in range(4):
        outs[s][...] = dot_nt(dpairs[s * length : (s + 1) * length], weight[:, width:]).astype(bf16)
    base[...] = delta[...] + dot_nt(query_low[...], weight[:, :width])


def fold(keep, got, small, split, after, present=(), cost=30):
    count, width = keep.shape
    half = count // 2 if split else count
    extra = 0 if small is None else SMALL_ROWS
    args = [keep, got] + ([] if small is None else [small])
    outs = [jax.ShapeDtypeStruct((half, width), bf16)]
    separate = split or extra
    if separate:
        outs.append(jax.ShapeDtypeStruct((half + extra, width), bf16))
    if extra:
        outs.append(jax.ShapeDtypeStruct((SMALL_ROWS, width), bf16))

    def kernel(*refs):
        mine, other = refs[0], refs[1]
        results = list(refs[len(args) :])
        kept = (mine[:half].astype(f32) + other[:half].astype(f32)).astype(bf16)
        results.pop(0)[...] = kept
        onward = results.pop(0) if separate else None
        if split:
            onward[:half] = (
                mine[half:count].astype(f32) + other[half:count].astype(f32)
            ).astype(bf16)
        elif separate:
            onward[:half] = kept
        if extra:
            total = (refs[2][...].astype(f32) + other[count:].astype(f32)).astype(bf16)
            results.pop(0)[...] = total
            if separate:
                onward[half:] = total

    res, token = call(
        kernel, outs, args, after=after, present=present, cost=cost, limit=SMALL_LIMIT
    )
    res = list(res)
    kept = res.pop(0)
    onward = res.pop(0) if separate else kept
    return kept, onward, (res.pop(0) if extra else None), token


def add_rows(parts, rows, after, present=(), front=None):
    ahead = 0 if front is None else front.shape[0]

    def kernel(*refs):
        total = 0.0
        for (_, row), ref in zip(parts, refs, strict=False):
            total = total + ref[row : row + rows].astype(f32)
        if ahead:
            refs[-1][:ahead] = refs[len(parts)][...]
        refs[-1][ahead:] = total.astype(bf16)

    outs = [jax.ShapeDtypeStruct((ahead + rows, parts[0][0].shape[1]), bf16)]
    args = [a for a, _ in parts] + ([] if front is None else [front])
    (whole,), token = call(kernel, outs, args, after=after, present=present, cost=FOLD / 3,
                           limit=SMALL_LIMIT)
    return whole, token


def hold(value, after=(), present=(), cost=1):
    any_space = pl.BlockSpec(memory_space=pl.ANY)
    extra = [*after, *present]
    return pl.pallas_call(
        lambda *refs: None,
        out_shape=jax.ShapeDtypeStruct(value.shape, value.dtype),
        in_specs=[any_space] * (1 + len(extra)),
        out_specs=any_space,
        input_output_aliases={0: 0},
        compiler_params=pltpu.CompilerParams(vmem_limit_bytes=1024 * 1024),
        cost_estimate=taking(cost),
    )(value, *extra)


def join(parts, after, present=(), cost=30):
    count = sum(part.shape[0] for part in parts)

    def kernel(*refs):
        position = 0
        for part in refs[: len(parts)]:
            refs[-1][position : position + part.shape[0]] = part[...]
            position += part.shape[0]

    outs = [jax.ShapeDtypeStruct((count, parts[0].shape[1]), bf16)]
    (whole,), token = call(
        kernel, outs, list(parts), after=after, present=present, cost=cost,
        limit=SMALL_LIMIT,
    )
    return whole, token


ORDER = (
    "A L B A~", "B~ L A L", "B A L A", "B L m B", "x L A fA", "L i B+L+i+m fB", "L fL",
)
FOLD = 30
SMALL_LIMIT = 24
MIB = 1024 * 1024
SMALL_COST = 0.1
K4B = 0.1
SIDE = "B"


class Chain:
    def __init__(self, keep, away, small, rows, seq):
        self.rows, self.seq = rows, seq
        self.core = [(r * seq + z, (r ^ 1) * seq + z) for r in range(rows) for z in range(seq)]
        self.keep, self.small = keep, small
        self.got = send(away, self.core)
        self.steps = len(bit_orders(rows)[0])
        self.k = 0
        self.mark = None
        self.mine = self.other = None

    def step(self, after=(), present=(), cost=30):
        k, n = self.k, self.steps
        self.k += 1
        if k <= n:
            self.keep, onward, self.small, self.mark = fold(
                self.keep, self.got, self.small, k < n - 1, after, present, cost
            )
            if k < n:
                self.got = send(onward, step_route(self.rows, self.seq, k))
            else:
                self.mine, self.other = [self.keep], [send(onward, self.core)]
                self.got = send(self.keep, step_route(self.rows, self.seq, n - 2))
        else:
            back = 2 * n - 2 - k
            if back < 0 and after:
                self.got = hold(self.got, after, present, cost)
            self.mine.append(self.got)
            self.other.append(send(self.got, self.core))
            if back >= 0:
                whole, self.mark = join(self.mine, after, present, cost)
                self.got = send(whole, step_route(self.rows, self.seq, back))

    @property
    def count(self):
        return 2 * self.steps


def place_parts(number, groups, wide, piece, half):
    core = number[0]
    for group, (top, low) in enumerate(((core, number[1]), (1 - core, number[2]))):
        position = 0
        for part in groups[group]:
            for t in range(part.shape[0] // piece):
                start = pl.multiple_of((((position + t) ^ low) + top * half) * piece, 16)
                wide[pl.ds(start, piece)] = part[t * piece : (t + 1) * piece].astype(f32)
            position += part.shape[0] // piece


CHUNK = 256


def finish_kernel(number, *refs, parts, piece, half, layout, moves, smalls, came):
    groups = (refs[:parts], refs[parts : 2 * parts])
    refs = list(refs[2 * parts :])
    if smalls:
        small, count = refs.pop(0), groups[0][0].shape[0]
        small_far = groups[1][0][count:]
    came, refs = refs[:came], refs[came:]
    sums, refs = refs[: len(layout)], refs[len(layout) :]
    small_out, refs = refs[: len(smalls)], refs[len(smalls) :]
    move_out, refs = refs[: len(moves)], refs[len(moves) :]
    token, wide, both, out_sems = refs
    copies = []

    def out(source, target):
        copies.append(pltpu.make_async_copy(source, target, out_sems.at[len(copies)]))
        copies[-1].start()

    place_parts(number, groups, wide, piece, half)
    row = 0
    for target, blocks in zip(sums, layout, strict=True):
        for to_row, to_column, count in blocks:
            for c in range(0, count, CHUNK):
                out(
                    wide.at[pl.ds(row + c, CHUNK)],
                    target.at[pl.ds(to_row + c, CHUNK), pl.ds(to_column, wide.shape[1])],
                )
            row = row + count
    for pieces, target in zip(moves, move_out, strict=True):
        for i, row, rows, column in pieces:
            out(came[i].at[pl.ds(row, rows)], target.at[:, pl.ds(column, came[i].shape[1])])
    if smalls:
        both[...] = 0.5 * (small[...].astype(f32) + small_far.astype(f32))
        for (first, count), target in zip(smalls, small_out, strict=True):
            for i in range(count):
                width = both.shape[1]
                out(both.at[pl.ds(first + i, 1)], target.at[:, pl.ds(i * width, width)])
    token[...] = jnp.zeros_like(token)
    for copy in copies:
        copy.wait()


def finish(number, chain, piece, half, shapes, layout, came=(), moves=(),
           smalls=(), after=(), present=(), cost=6):
    parts = len(chain.mine)
    width = chain.mine[0].shape[1]
    total = 2 * half * piece
    hbm = pl.BlockSpec(memory_space=pltpu.HBM)
    vmem = pl.BlockSpec(memory_space=pltpu.VMEM)
    extra = [chain.small] if smalls else []
    count = total // CHUNK + sum(len(m) for m in moves) + sum(n for _, n in smalls)
    moved = [jax.ShapeDtypeStruct((m[0][2], len(m) * width), bf16) for m in moves]

    def kernel(*refs):
        given = 1 + 2 * parts + len(extra) + len(came)
        finish_kernel(
            *refs[:given], *refs[given + len(after) + len(present) :],
            parts=parts, piece=piece, half=half, layout=layout, moves=moves, smalls=smalls,
            came=len(came),
        )

    res = pl.pallas_call(
        kernel,
        in_specs=[pl.BlockSpec(memory_space=pltpu.SMEM)]
        + [vmem] * (2 * parts + len(extra) + len(came) + len(after)) + [hbm] * len(present),
        out_specs=[hbm] * (len(shapes) + len(smalls) + len(moves)) + [vmem],
        out_shape=[jax.ShapeDtypeStruct(s, f32) for s in shapes]
        + [jax.ShapeDtypeStruct((1, n * width), f32) for _, n in smalls]
        + moved + [TOKEN],
        scratch_shapes=[
            pltpu.VMEM((total, width), f32),
            pltpu.VMEM((SMALL_ROWS, width), f32),
            pltpu.SemaphoreType.DMA((count,)),
        ],
        compiler_params=pltpu.CompilerParams(vmem_limit_bytes=20 * MIB),
        cost_estimate=taking(cost),
    )(number, *chain.mine, *chain.other, *extra, *came, *after, *present)
    return res[:-1], res[-1]


def pack(inputs, target, source, vectors):
    length, width = inputs.shape
    count = sum(v.shape[1] // width for v in vectors)
    outs = [
        jax.ShapeDtypeStruct((length + 16, width), bf16), jax.ShapeDtypeStruct((count, width), f32)
    ]

    def kernel(given, target, source, *refs):
        out, stacked = refs[-2:]
        out[:length] = given[...]
        out[length:] = jnp.zeros_like(out[length:])
        labels = jnp.concatenate([target[...], source[...]], axis=0)
        out[length : length + 2, :length] = labels.astype(f32).astype(bf16)
        row = 0
        for vector in refs[:-2]:
            for c in range(vector.shape[1] // width):
                stacked[row : row + 1] = vector[:, c * width : (c + 1) * width]
                row += 1

    args = [inputs, target, source, *vectors]
    return call(kernel, outs, args, lazy=range(len(args)), cost=2, limit=60)


def piece_rows(count, pieces):
    return -(-count // (pieces * 16)) * 16


def shards(
    inputs, memory, target_segments, memory_segments, self_project, self_query_bias,
    self_value_bias, self_output, self_output_bias, self_norm_gain, self_norm_bias, cross_query,
    cross_query_bias, cross_output, cross_output_bias, cross_norm_gain, cross_norm_bias,
    expand_weight, expand_bias, contract_weight, contract_bias, final_norm_gain, final_norm_bias,
    cotangent,
):
    rows, seq = lax.axis_size("rows"), lax.axis_size("seq")
    r, z = lax.axis_index("rows"), lax.axis_index("seq")
    _, length, width = inputs.shape
    hidden = expand_weight.shape[1]
    factor = float(width // HEADS) ** (-0.5)
    home = home_route(rows, seq)
    core = [(a * seq + b, (a ^ 1) * seq + b) for a in range(rows) for b in range(seq)]
    side = [(a * seq + b, a * seq + (b ^ 1)) for a in range(rows) for b in range(seq)]
    orders = bit_orders(rows)
    half = 2 ** (len(orders[0]) - 1)
    lows = [low_number(rows, order[:-1], r, z) for order in orders]
    is_one = (r & 1) == 1
    place = (z & 1) + 2 * (r & 1)
    number = jnp.stack([
        r & 1, jnp.where(is_one, lows[1], lows[0]), jnp.where(is_one, lows[0], lows[1]), place,
    ]).astype(jnp.int32)

    def line(vector):
        return vector.reshape(1, -1)

    m0 = send(memory[0], home)
    (packed, vectors), tick = pack(
        inputs[0], target_segments, memory_segments,
        [
            line(v)
            for v in (
                self_query_bias, self_value_bias, self_output_bias, self_norm_gain,
                self_norm_bias, cross_query_bias, cross_output_bias, cross_norm_gain,
                cross_norm_bias, contract_bias, final_norm_gain, final_norm_bias, expand_bias,
            )
        ],
    )
    x0 = send(packed, home)
    _, tick = call(lambda: None, [], [], cost=30, after=(tick,), limit=1)
    m0 = hold(m0, cost=20)
    x1 = send(x0, side)
    x2 = send(x0, core)
    m1 = send(m0, side)
    m2 = send(m0, core)
    x3 = send(x1, core)
    pulled = send(cotangent[0], home)

    def shape(*dims, dtype=f32):
        return jax.ShapeDtypeStruct(dims, dtype)

    def low(*dims):
        return jax.ShapeDtypeStruct(dims, bf16)

    vmem = pl.BlockSpec(memory_space=pltpu.VMEM)
    any_space = pl.BlockSpec(memory_space=pl.ANY)
    bias_space = pltpu.VMEM((length, 4 * length), f32)
    bias_turned = pltpu.VMEM((4 * length, length), f32)

    (pairs, query, self_result, self_logs, normed1, scale1, asked, marks), token = call(
        functools.partial(self_kernel, factor=factor),
        [
            low(4 * length, 2 * width), low(length, width), shape(length, width),
            shape(length, PAIR), shape(length, width), shape(length, PAIR), low(length, width),
            shape(8, 4 * length),
        ],
        [number[3:4], x0, x1, x2, x3, self_project, self_output, cross_query, vectors],
        scratch=[bias_space],
        lazy=[5, 8, 1, 2, 3, 4, 6, 7],
        cost=9,
        after=(tick,),
    )

    m1 = hold(m1, (), cost=20)
    m3 = send(m1, core)

    piece_a = piece_rows(hidden, 2 * half)
    piece_b = piece_rows(hidden + width, 2 * half)
    (
        output, keep_a, away_a, keep_b, away_b, small, cross_delta, crossed_pull, cross_result,
        cross_logs,
    ), _ = call(
        functools.partial(cross_kernel, factor=factor, piece_a=piece_a, piece_b=piece_b),
        [
            low(length, width), low(half * piece_a, width), low(half * piece_a, width),
            low(half * piece_b, width), low(half * piece_b, width),
            shape(SMALL_ROWS, width), shape(length, width), low(length, width),
            shape(length, width), shape(length, PAIR),
        ],
        [
            number, asked, m0, m1, m2, m3, marks, normed1, cross_output, expand_weight,
            contract_weight, vectors, pulled,
        ],
        scratch=[
            bias_space,
            pltpu.VMEM((2 * half * piece_a, width), bf16),
            pltpu.VMEM((2 * half * piece_b, width), bf16),
        ],
        lazy=[2, 3, 4, 5, 8, 9, 10, 12],
        cost=15,
        limit=44,
    )
    chains = {
        "A": Chain(keep_a, away_a, None, rows, seq),
        "B": Chain(keep_b, away_b, None, rows, seq),
    }

    (mem_near0, mem_near1, mem_far, asked_low), token = call(
        functools.partial(cross_back_kernel, factor=factor),
        [low(2 * length, width), low(2 * length, width), low(4 * length, width),
         low(length, width)],
        [asked, m0, m1, m2, m3, marks, crossed_pull, cross_result, cross_logs],
        scratch=[bias_turned],
        lazy=range(1, 5),
        cost=8,
    )
    for name in "AB":
        chains[name].step((token,))
        token = chains[name].mark
    mem_far = send(mem_far, core)

    (late, self_delta, mixed_pull, small), token = call(
        middle_kernel,
        [low(2 * width, width), shape(length, width), low(length, width),
         shape(SMALL_ROWS, width)],
        [
            asked_low, cross_delta, normed1, scale1, vectors, self_result, cross_query,
            self_output, small,
        ],
        lazy=[6, 7],
        cost=3,
        after=(token,),
    )
    onward, token = add_rows([(mem_near1, 0), (mem_far, 2 * length)], 2 * length, (token,))
    mem_got = send(onward, side)

    (dpairs, query_low), token = call(
        functools.partial(self_back_kernel, factor=factor),
        [low(4 * length, 2 * width), low(length, width)],
        [number[3:4], query, pairs, marks, mixed_pull, self_result, self_logs],
        scratch=[bias_turned],
        cost=8,
        after=(token,),
    )
    chains["A"].step((token,), (mem_got,) if SIDE == "A" else (), cost=SMALL_COST)
    late_piece = piece_rows(5 * width, 2 * half)
    (late_keep, late_away), token = call(
        functools.partial(project_sums_kernel, piece=late_piece),
        [low(half * late_piece, width), low(half * late_piece + SMALL_ROWS, width)],
        [number, dpairs, query_low, x0, x1, x2, x3, late, small],
        scratch=[
            pltpu.VMEM((2 * half * late_piece, width), bf16),
            pltpu.VMEM((width, 4 * length), bf16),
        ],
        lazy=range(3, 7),
        cost=K4B,
        after=(chains["A"].mark,),
    )
    chains["B"].step((token,), (mem_got,) if SIDE == "B" else (), cost=SMALL_COST)
    (in_near0, in_near1, in_far, base), token = call(
        project_back_kernel,
        [low(length, width), low(length, width), low(2 * length, width), shape(length, width)],
        [dpairs, query_low, self_delta, self_project],
        lazy=[3],
        cost=3,
        after=(chains["B"].mark,),
    )
    chains["L"] = Chain(late_keep, late_away, late_away[-SMALL_ROWS:], rows, seq)
    in_far = send(in_far, core)

    steps = " ".join(ORDER).split()
    blocks = range(hidden // width)
    smalls = [(0, 1), (1, 1), (2, 1), (3, 1), (4, 1), (5, 1), (6, hidden // width)]
    smalls += [(i, 1) for i in range(10, 16)]
    if "m" in steps:
        home_parts = [
            [(0, 0, length, 0)], [(0, length, length, 0), (0, 2 * length, length, width)]
        ]
    else:
        home_parts = [[(0, 0, length, 0)], [(1, 0, length, 0), (2, 0, length, width)]]
    ends = {
        "A": dict(piece=piece_a, shapes=[(hidden, width)],
                  layout=[[(c * width, 0, width) for c in blocks]]),
        "B": dict(piece=piece_b, shapes=[(width, hidden), (width, width)],
                  layout=[[(0, c * width, width) for c in blocks], [(0, 0, width)]],
                  moves=home_parts),
        "L": dict(piece=late_piece, shapes=[(width, width), (width, width), (width, 3 * width)],
                  layout=[[(0, 0, width)], [(0, 0, width)],
                          [(0, c * width, width) for c in range(3)]],
                  moves=[[(0, 0, length, 0)]], smalls=smalls),
    }
    known, done = {}, {}
    for step in steps:
        name, *wanted = step.split("+")
        cost = 0.1 if name.endswith("~") else FOLD
        name = name.rstrip("~")
        present = tuple(chains[w].got if w in chains else known[w] for w in wanted)
        if name in chains:
            chains[name].step((token,), present, cost=cost)
            token = chains[name].mark
        elif name == "m":
            known["m"], token = add_rows(
                [(mem_near0, 0), (mem_far, 0), (mem_got, 0)], 2 * length, (token,), present,
                front=output,
            )
            known["m"] = send(known["m"], home)
        elif name == "o":
            known["o"] = send(output, home)
        elif name in ("k", "v"):
            row = 0 if name == "k" else length
            known[name], token = add_rows(
                [(mem_near0, row), (mem_far, row), (mem_got, row)], length, (token,), present
            )
            known[name] = send(known[name], home)
        elif name == "x":
            onward, token = add_rows([(in_near1, 0), (in_far, length)], length, (token,), present)
            in_got = send(onward, side)
        elif name == "i":
            known["i"], token = add_rows(
                [(base, 0), (in_near0, 0), (in_far, 0), (in_got, 0)], length, (token,), present
            )
            known["i"] = send(known["i"], home)
        else:
            end = ends[name[1]]
            if name == "fB":
                end["came"] = [known[c] for c in ("m" if "m" in known else "okv")]
            if name == "fL":
                end["came"] = [known["i"]]
            done[name[1]], token = finish(
                number, chains[name[1]], half=half, after=(token,), present=present, **end
            )
    (gradient_contract,) = done["A"]
    gradient_expand, gradient_cross_output, output, memory_gradient = done["B"]
    (
        gradient_cross_query, gradient_self_output, gradient_self_project, gradient_final_gain,
        gradient_final_bias, gradient_contract_bias, gradient_cross_gain, gradient_cross_bias,
        gradient_cross_output_bias, gradient_expand_bias, gradient_cross_query_bias,
        gradient_self_gain, gradient_self_bias, gradient_self_output_bias, gradient_query_bias,
        gradient_value_bias, input_gradient,
    ) = done["L"]

    return (
        output[None],
        input_gradient[None],
        memory_gradient[None],
        gradient_self_project,
        gradient_query_bias.reshape(-1),
        gradient_value_bias.reshape(-1),
        gradient_self_output,
        gradient_self_output_bias.reshape(-1),
        gradient_self_gain.reshape(-1),
        gradient_self_bias.reshape(-1),
        gradient_cross_query,
        gradient_cross_query_bias.reshape(-1),
        gradient_cross_output,
        gradient_cross_output_bias.reshape(-1),
        gradient_cross_gain.reshape(-1),
        gradient_cross_bias.reshape(-1),
        gradient_expand,
        gradient_expand_bias.reshape(-1),
        gradient_contract,
        gradient_contract_bias.reshape(-1),
        gradient_final_gain.reshape(-1),
        gradient_final_bias.reshape(-1),
    )


def solution(mesh):
    tokens = P("rows", "seq", None)
    in_specs = (tokens, tokens, P("rows", "seq"), P("rows", "seq")) + (P(),) * 19 + (tokens,)
    out_specs = (tokens,) * 3 + (P(),) * 19
    return jax.shard_map(shards, mesh=mesh, in_specs=in_specs, out_specs=out_specs, check_vma=False)
```

```python
import functools

import jax
import jax.numpy as jnp
from jax import lax
from jax.experimental import pallas as pl
from jax.experimental.pallas import tpu as pltpu
from jax.sharding import PartitionSpec as P

HEADS = 8
PAIR = 128
SMALL_ROWS = 16
masked_score = -1e30
epsilon = 1e-05
f32 = jnp.float32
bf16 = jnp.bfloat16
BOTH = ("rows", "seq")


def dot(left, right):
    return jnp.dot(left, right, preferred_element_type=f32)


def dot_nt(left, right):
    return lax.dot_general(left, right, (((1,), (1,)), ((), ())), preferred_element_type=f32)


def dot_tn(left, right):
    return lax.dot_general(left, right, (((0,), (0,)), ((), ())), preferred_element_type=f32)


def norm_forward(value, gain, shift):
    center = jnp.mean(value, axis=-1, keepdims=True)
    centred = value - center
    scale = lax.rsqrt(jnp.mean(centred * centred, axis=-1, keepdims=True) + epsilon)
    normed = centred * scale
    return normed * gain + shift, normed, scale


def norm_backward(incoming, normed, scale, gain):
    weighted = incoming * gain
    spread = weighted - jnp.mean(weighted, axis=-1, keepdims=True)
    spread = spread - normed * jnp.mean(weighted * normed, axis=-1, keepdims=True)
    return scale * spread, column_total(incoming * normed), column_total(incoming)


def column_total(value):
    return jnp.sum(value.astype(f32), axis=0, keepdims=True)


def head_lanes(shape, h):
    lane = lax.broadcasted_iota(jnp.int32, shape, 1)
    return (lane < 64) if h == 0 else (lane >= 64)


def only_head(value, h):
    return jnp.where(head_lanes(value.shape, h), value, jnp.zeros_like(value))


def flat_pairs(rows, seq, partner):
    return [(r * seq + z, partner(r, z)) for r in range(rows) for z in range(seq)]


def home_route(rows, seq):
    def partner(r, z):
        if (r & 1) == z // 2:
            return r * seq + z
        return (r ^ 1) * seq + (z ^ 2)

    return flat_pairs(rows, seq, partner)


def bit_orders(rows):
    count = rows.bit_length() - 2
    bits = [("r", 1 << (k + 1)) for k in range(count)]
    tail = [("z", 1), ("z", 2)]
    return bits + tail, bits[::-1] + tail


def step_route(rows, seq, k):
    orders = bit_orders(rows)

    def partner(r, z):
        kind, mask = orders[r & 1][k]
        return (r ^ mask) * seq + z if kind == "r" else r * seq + (z ^ mask)

    return flat_pairs(rows, seq, partner)


def low_number(rows, order, r, z):
    number = jnp.int32(0)
    for kind, mask in order:
        bit = jnp.where(((r if kind == "r" else z) & mask) != 0, 1, 0)
        number = number * 2 + bit
    return number


def send(value, route):
    return lax.ppermute(value, BOTH, route)


def taking(us):
    return pl.CostEstimate(
        flops=int(us * 1.15e9), bytes_accessed=int(us * 3.6e6), transcendentals=0
    )


class Lazy:
    def __init__(self, far, near, sem):
        self.copy, self.near, self.waiting = pltpu.make_async_copy(far, near, sem), near, True
        self.copy.start()

    @property
    def shape(self):
        return self.near.shape

    def __getitem__(self, index):
        if self.waiting:
            self.copy.wait()
            self.waiting = False
        return self.near[index]


TOKEN = jax.ShapeDtypeStruct((8, 128), f32)


def call(kernel, outs, args, scratch=(), lazy=(), out_specs=None, cost=None, after=(), present=(),
         limit=24):
    vmem = pl.BlockSpec(memory_space=pltpu.VMEM)
    smem = pl.BlockSpec(memory_space=pltpu.SMEM)
    hbm = pl.BlockSpec(memory_space=pltpu.HBM)
    count = len(args)
    lazy = list(lazy)

    def spec(i, arg):
        if i in lazy:
            return hbm
        return smem if arg.dtype == jnp.int32 and arg.ndim == 1 else vmem

    def inner(*refs):
        given = list(refs[:count])
        rest = refs[count + len(after) + len(present) :]
        results, token, held = rest[: len(outs)], rest[len(outs)], rest[len(outs) + 1 :]
        near, held = held[: len(lazy)], held[len(lazy) :]
        if lazy:
            sems, held = held[0], held[1:]
            for k, i in enumerate(lazy):
                given[i] = Lazy(given[i], near[k], sems.at[k])
        kernel(*given, *results, *held)
        for i in lazy:
            if given[i].waiting:
                given[i].copy.wait()
        token[...] = jnp.zeros_like(token)

    spaces = [pltpu.VMEM(args[i].shape, args[i].dtype) for i in lazy]
    if lazy:
        spaces.append(pltpu.SemaphoreType.DMA((len(lazy),)))
    res = pl.pallas_call(
        inner,
        out_shape=list(outs) + [TOKEN],
        in_specs=[spec(i, a) for i, a in enumerate(args)]
        + [vmem] * len(after) + [hbm] * len(present),
        out_specs=(out_specs if out_specs is not None else [vmem] * len(outs)) + [vmem],
        scratch_shapes=spaces + list(scratch),
        compiler_params=pltpu.CompilerParams(vmem_limit_bytes=limit * 1024 * 1024),
        cost_estimate=None if cost is None else taking(cost),
    )(*args, *after, *present)
    return res[:-1], res[-1]


def mask_bias(bias, place, query_labels, key_labels, length, causal):
    asking = jnp.broadcast_to(query_labels, (length, length)).T
    for s in range(4):
        same = asking == key_labels[s]
        if causal:
            query = place * length + lax.broadcasted_iota(jnp.int32, (length, length), 0)
            key = (place ^ s) * length + lax.broadcasted_iota(jnp.int32, (length, length), 1)
            same = same & (key <= query)
        bias[:, s * length : (s + 1) * length] = jnp.where(same, 0.0, masked_score)


def attend(query, keys, values, bias, factor, result, logs):
    length, width = query.shape
    lane = lax.broadcasted_iota(jnp.int32, (length, PAIR), 1)
    log_all = jnp.zeros((length, PAIR), f32)
    for j in range(width // PAIR):
        columns = slice(j * PAIR, (j + 1) * PAIR)
        pair = query[:, columns] * jnp.asarray(factor, bf16)
        key, value = keys(j), values(j)
        halves = []
        for h in range(2):
            scores = dot_nt(only_head(pair, h), key) + bias[...]
            peak = jnp.max(scores, axis=-1, keepdims=True)
            raised = jnp.exp(scores - peak)
            total = jnp.sum(raised, axis=-1, keepdims=True)
            halves.append(dot(raised.astype(bf16), value) / total)
            log_all = jnp.where(lane == 2 * j + h, peak + jnp.log(total), log_all)
        result[:, columns] = jnp.where(lane < 64, halves[0], halves[1])
    logs[...] = log_all


def head_rows(query, result, pull, length, width):
    lane = lax.broadcasted_iota(jnp.int32, (length, PAIR), 1)
    sums = jnp.zeros((length, PAIR), f32)
    for j in range(width // PAIR):
        columns = slice(j * PAIR, (j + 1) * PAIR)
        product = pull[:, columns].astype(f32) * result[:, columns]
        for h in range(2):
            total = jnp.sum(only_head(product, h), axis=-1, keepdims=True)
            sums = jnp.where(lane == 2 * j + h, total, sums)
    return sums.T


def mask_bias_turned(bias, place, query_labels, key_labels, length, causal):
    for s in range(4):
        holding = jnp.broadcast_to(key_labels[s], (length, length)).T
        same = holding == query_labels
        if causal:
            query = place * length + lax.broadcasted_iota(jnp.int32, (length, length), 1)
            key = (place ^ s) * length + lax.broadcasted_iota(jnp.int32, (length, length), 0)
            same = same & (key <= query)
        bias[s * length : (s + 1) * length] = jnp.where(same, 0.0, masked_score)


def attend_back(query, keys, values, bias, factor, result, logs, pull, dq, store):
    length, width = query.shape
    deltas = head_rows(query, result, pull, length, width)
    totals = logs[...].T
    for j in range(width // PAIR):
        columns = slice(j * PAIR, (j + 1) * PAIR)
        pair = query[:, columns] * jnp.asarray(factor, bf16)
        wanted = pull[:, columns]
        key, value = keys(j), values(j)
        key_turned = key.T
        dkey, dvalue, dquery = 0.0, 0.0, []
        for h in range(2):
            row = slice(2 * j + h, 2 * j + h + 1)
            asking, pulling = only_head(pair, h), only_head(wanted, h)
            chance = jnp.exp(dot_nt(key, asking) + bias[...] - totals[row])
            slope = (chance * (dot_nt(value, pulling) - deltas[row])).astype(bf16)
            dquery.append(dot(key_turned[h * 64 : h * 64 + 64], slope))
            dkey = dkey + dot(slope, asking)
            dvalue = dvalue + dot(chance.astype(bf16), pulling)
        dq[:, columns] = (jnp.concatenate(dquery, axis=0).T * factor).astype(bf16)
        store(j, dkey.astype(bf16), dvalue.astype(bf16))


def rows_of(vectors, first, count):
    return [vectors[i : i + 1] for i in range(first, first + count)]


def row_labels(marks, row, length):
    return [marks[row : row + 1, s * length : (s + 1) * length] for s in range(4)]


def self_kernel(
    place, x0, x1, x2, x3, weight, out_weight, ask_weight, vectors,
    pairs, query, result, logs, normed, scale, asked, marks, bias, factor,
):
    length, width = query.shape
    blocks = (x0, x1, x2, x3)
    query_bias, value_bias, out_bias, gain, shift, ask_bias = rows_of(vectors, 0, 6)
    for s, block in enumerate(blocks):
        both = dot(block[:length], weight[:, width:])
        rows = slice(s * length, (s + 1) * length)
        pairs[rows, :width] = both[:, :width].astype(bf16)
        pairs[rows, width:] = (both[:, width:] + value_bias).astype(bf16)
    query[...] = (dot(x0[:length], weight[:, :width]) + query_bias).astype(bf16)
    for s, block in enumerate(blocks):
        columns = slice(s * length, (s + 1) * length)
        marks[:, columns] = block[length : length + 8, :length].astype(f32)
    labels = row_labels(marks, 0, length)
    mask_bias(bias, place[0], labels[0], labels, length, True)
    attend(
        query,
        lambda j: pairs[:, j * PAIR : (j + 1) * PAIR],
        lambda j: pairs[:, width + j * PAIR : width + (j + 1) * PAIR],
        bias, factor, result, logs,
    )
    mixed = result[...].astype(bf16)
    before = x0[:length].astype(f32) + dot(mixed, out_weight[...]) + out_bias
    first, normed[...], spread = norm_forward(before, gain, shift)
    scale[...] = jnp.broadcast_to(spread, scale.shape)
    asked[...] = (dot(first.astype(bf16), ask_weight[...]) + ask_bias).astype(bf16)


def memory_views(blocks, length, width):
    def keys(j):
        return jnp.concatenate([m[:length, j * PAIR : (j + 1) * PAIR] for m in blocks], axis=0)

    def values(j):
        return jnp.concatenate(
            [m[:length, width + j * PAIR : width + (j + 1) * PAIR] for m in blocks], axis=0
        )

    return keys, values


def cross_kernel(
    number, asked, m0, m1, m2, m3, marks, normed1, out_weight, grow, shrink, vectors, cotangent,
    output, keep_a, away_a, keep_b, away_b, small, delta, pull, result, logs,
    bias, sums_a, sums_b, factor, piece_a, piece_b,
):
    length, width = asked.shape
    hidden = grow.shape[1]
    blocks = (m0, m1, m2, m3)
    gain1, shift1 = rows_of(vectors, 3, 2)
    out_bias, gain2, shift2, shrink_bias, gain3, shift3 = rows_of(vectors, 6, 6)
    grow_bias = jnp.concatenate(rows_of(vectors, 12, hidden // width), axis=1)
    asking, labels = row_labels(marks, 0, length)[0], row_labels(marks, 1, length)
    mask_bias(bias, None, asking, labels, length, False)
    keys, values = memory_views(blocks, length, width)
    attend(asked, keys, values, bias, factor, result, logs)
    crossed = result[...].astype(bf16)
    first = normed1[...] * gain1 + shift1
    before = first + dot(crossed, out_weight[...]) + out_bias
    second, normed2, scale2 = norm_forward(before, gain2, shift2)
    second_low = second.astype(bf16)
    inner = dot(second_low, grow[...]) + grow_bias
    gate = 1.0 / (1.0 + jnp.exp(-inner))
    active = (inner * gate).astype(bf16)
    before = second + dot(active, shrink[...]) + shrink_bias
    final, normed3, scale3 = norm_forward(before, gain3, shift3)
    output[...] = final.astype(bf16)

    incoming = cotangent[...].astype(f32)
    third, gain3_sum, shift3_sum = norm_backward(incoming, normed3, scale3, gain3)
    shrink_low = third.astype(bf16)
    sums_a[0:hidden] = dot_tn(active, shrink_low).astype(bf16)
    fill_up(sums_a, hidden)
    slope = gate * (1.0 + inner * (1.0 - gate))
    grow_low = (dot_nt(shrink_low, shrink[...]) * slope).astype(bf16)
    grown = dot_tn(second_low, grow_low).astype(bf16)
    for c in range(hidden // width):
        sums_b[c * width : (c + 1) * width] = grown[:, c * width : (c + 1) * width]
    second_gradient = third + dot_nt(grow_low, grow[...])
    cross_delta, gain2_sum, shift2_sum = norm_backward(
        second_gradient, normed2, scale2, gain2
    )
    delta[...] = cross_delta
    cross_low = cross_delta.astype(bf16)
    sums_b[hidden : hidden + width] = dot_tn(crossed, cross_low).astype(bf16)
    fill_up(sums_b, hidden + width)
    spread_pieces(number, sums_a, keep_a, away_a, piece_a)
    spread_pieces(number, sums_b, keep_b, away_b, piece_b)
    pull[...] = dot_nt(cross_low, out_weight[...]).astype(bf16)
    grow_sum = column_total(grow_low)
    rows = [gain3_sum, shift3_sum, column_total(shrink_low), gain2_sum, shift2_sum,
            column_total(cross_low)]
    rows += [grow_sum[:, c * width : (c + 1) * width] for c in range(hidden // width)]
    rows += [jnp.zeros((SMALL_ROWS - len(rows), width), f32)]
    small[...] = jnp.concatenate(rows, axis=0)


def fill_up(sums, count):
    if sums.shape[0] > count:
        sums[count:] = jnp.zeros_like(sums[count:])


def spread_pieces(number, sums, keep, away, piece):
    half = sums.shape[0] // piece // 2
    core, mine, other = number[0], number[1], number[2]
    for q in range(half):
        for target, top, low in ((keep, core, mine), (away, 1 - core, other)):
            start = pl.multiple_of(((q ^ low) + top * half) * piece, 16)
            target[q * piece : (q + 1) * piece] = sums[pl.ds(start, piece)]


def cross_back_kernel(
    asked, m0, m1, m2, m3, marks, pull, result, logs, near0, near1, far, asked_low, bias, factor
):
    length, width = asked.shape
    blocks = (m0, m1, m2, m3)
    asking, labels = row_labels(marks, 0, length)[0], row_labels(marks, 1, length)
    mask_bias_turned(bias, None, asking, labels, length, False)
    keys, values = memory_views(blocks, length, width)
    outs = ((near0, 0), (near1, 0), (far, 0), (far, 2 * length))

    def store(j, dkey, dvalue):
        for k, part in enumerate((dkey, dvalue)):
            for s, (out, row) in enumerate(outs):
                start = row + k * length
                out[start : start + length, j * PAIR : (j + 1) * PAIR] = part[
                    s * length : (s + 1) * length
                ]

    attend_back(asked, keys, values, bias, factor, result, logs, pull, asked_low, store)


def middle_kernel(
    asked_low, cross_delta, normed1, scale1, vectors, self_result, ask_weight,
    self_out_weight, small_in, late, delta, mixed_pull, small,
):
    width = asked_low.shape[1]
    gain1, shift1 = rows_of(vectors, 3, 2)
    normed = normed1[...]
    first_low = (normed * gain1 + shift1).astype(bf16)
    first_gradient = cross_delta[...] + dot_nt(asked_low[...], ask_weight[...])
    self_delta, gain_sum, shift_sum = norm_backward(
        first_gradient, normed, scale1[:, 0:1], gain1
    )
    delta[...] = self_delta
    self_low = self_delta.astype(bf16)
    mixed_pull[...] = dot_nt(self_low, self_out_weight[...]).astype(bf16)
    late[0:width] = dot_tn(first_low, asked_low[...]).astype(bf16)
    late[width : 2 * width] = dot_tn(self_result[...].astype(bf16), self_low).astype(bf16)
    small[...] = small_in[...]
    small[10:14] = jnp.concatenate(
        [column_total(asked_low[...]), gain_sum, shift_sum, column_total(self_low)], axis=0
    )


def self_back_kernel(
    place, query, pairs, marks, pull, result, logs, dpairs, query_low, bias, factor
):
    length, width = query.shape
    labels = row_labels(marks, 0, length)
    mask_bias_turned(bias, place[0], labels[0], labels, length, True)

    def store(j, dkey, dvalue):
        dpairs[:, j * PAIR : (j + 1) * PAIR] = dkey
        dpairs[:, width + j * PAIR : width + (j + 1) * PAIR] = dvalue

    attend_back(
        query,
        lambda j: pairs[:, j * PAIR : (j + 1) * PAIR],
        lambda j: pairs[:, width + j * PAIR : width + (j + 1) * PAIR],
        bias, factor, result, logs, pull, query_low, store,
    )


def project_sums_kernel(
    number, dpairs, query_low, x0, x1, x2, x3, late, small_in,
    keep, away, sums, turned, piece,
):
    length, width = query_low.shape
    done = late.shape[0]
    sums[0:done] = late[...]
    for s, block in enumerate((x0, x1, x2, x3)):
        turned[:, s * length : (s + 1) * length] = block[:length].T
    sums[done : done + width] = dot(turned[:, :length], query_low[...]).astype(bf16)
    for half in range(2):
        total = dot(turned[...], dpairs[:, half * width : (half + 1) * width])
        sums[done + (1 + half) * width : done + (2 + half) * width] = total.astype(bf16)
    fill_up(sums, done + 3 * width)
    spread_pieces(number, sums, keep, away, piece)
    rows = keep.shape[0]
    sums_small = [column_total(query_low[...]), column_total(dpairs[:, width:])]
    whole = jnp.concatenate([small_in[:14]] + sums_small, axis=0)
    away[rows : rows + SMALL_ROWS] = whole.astype(bf16)


def project_back_kernel(dpairs, query_low, delta, weight, near0, near1, far, base):
    length, width = query_low.shape
    outs = (near0.at[...], near1.at[...], far.at[0:length], far.at[length : 2 * length])
    for s in range(4):
        outs[s][...] = dot_nt(dpairs[s * length : (s + 1) * length], weight[:, width:]).astype(bf16)
    base[...] = delta[...] + dot_nt(query_low[...], weight[:, :width])


def fold(keep, got, small, split, after, present=(), cost=30):
    count, width = keep.shape
    half = count // 2 if split else count
    extra = 0 if small is None else SMALL_ROWS
    args = [keep, got] + ([] if small is None else [small])
    outs = [jax.ShapeDtypeStruct((half, width), bf16)]
    separate = split or extra
    if separate:
        outs.append(jax.ShapeDtypeStruct((half + extra, width), bf16))
    if extra:
        outs.append(jax.ShapeDtypeStruct((SMALL_ROWS, width), bf16))

    def kernel(*refs):
        mine, other = refs[0], refs[1]
        results = list(refs[len(args) :])
        kept = (mine[:half].astype(f32) + other[:half].astype(f32)).astype(bf16)
        results.pop(0)[...] = kept
        onward = results.pop(0) if separate else None
        if split:
            onward[:half] = (
                mine[half:count].astype(f32) + other[half:count].astype(f32)
            ).astype(bf16)
        elif separate:
            onward[:half] = kept
        if extra:
            total = (refs[2][...].astype(f32) + other[count:].astype(f32)).astype(bf16)
            results.pop(0)[...] = total
            if separate:
                onward[half:] = total

    res, token = call(
        kernel, outs, args, after=after, present=present, cost=cost, limit=SMALL_LIMIT
    )
    res = list(res)
    kept = res.pop(0)
    onward = res.pop(0) if separate else kept
    return kept, onward, (res.pop(0) if extra else None), token


def add_rows(parts, rows, after, present=(), front=None):
    ahead = 0 if front is None else front.shape[0]

    def kernel(*refs):
        total = 0.0
        for (_, row), ref in zip(parts, refs, strict=False):
            total = total + ref[row : row + rows].astype(f32)
        if ahead:
            refs[-1][:ahead] = refs[len(parts)][...]
        refs[-1][ahead:] = total.astype(bf16)

    outs = [jax.ShapeDtypeStruct((ahead + rows, parts[0][0].shape[1]), bf16)]
    args = [a for a, _ in parts] + ([] if front is None else [front])
    (whole,), token = call(kernel, outs, args, after=after, present=present, cost=FOLD / 3,
                           limit=SMALL_LIMIT)
    return whole, token


def hold(value, after=(), present=(), cost=1):
    any_space = pl.BlockSpec(memory_space=pl.ANY)
    extra = [*after, *present]
    return pl.pallas_call(
        lambda *refs: None,
        out_shape=jax.ShapeDtypeStruct(value.shape, value.dtype),
        in_specs=[any_space] * (1 + len(extra)),
        out_specs=any_space,
        input_output_aliases={0: 0},
        compiler_params=pltpu.CompilerParams(vmem_limit_bytes=1024 * 1024),
        cost_estimate=taking(cost),
    )(value, *extra)


def join(parts, after, present=(), cost=30):
    count = sum(part.shape[0] for part in parts)

    def kernel(*refs):
        position = 0
        for part in refs[: len(parts)]:
            refs[-1][position : position + part.shape[0]] = part[...]
            position += part.shape[0]

    outs = [jax.ShapeDtypeStruct((count, parts[0].shape[1]), bf16)]
    (whole,), token = call(
        kernel, outs, list(parts), after=after, present=present, cost=cost,
        limit=SMALL_LIMIT,
    )
    return whole, token


ORDER = (
    "A L B x", "A~ B~ L A", "L i B A", "L A B L+i",
    "m B L A", "fA L B+L+i+m L", "fBL",
)
FOLD = 30
SMALL_LIMIT = 24
MIB = 1024 * 1024
SMALL_COST = 0.1
K4B = 0.1
SIDE = "B"


class Chain:
    def __init__(self, keep, away, small, rows, seq):
        self.rows, self.seq = rows, seq
        self.core = [(r * seq + z, (r ^ 1) * seq + z) for r in range(rows) for z in range(seq)]
        self.keep, self.small = keep, small
        self.got = send(away, self.core)
        self.steps = len(bit_orders(rows)[0])
        self.k = 0
        self.mark = None
        self.mine = self.other = None

    def step(self, after=(), present=(), cost=30):
        k, n = self.k, self.steps
        self.k += 1
        if k <= n:
            self.keep, onward, self.small, self.mark = fold(
                self.keep, self.got, self.small, k < n - 1, after, present, cost
            )
            if k < n:
                self.got = send(onward, step_route(self.rows, self.seq, k))
            else:
                self.mine, self.other = [self.keep], [send(onward, self.core)]
                self.got = send(self.keep, step_route(self.rows, self.seq, n - 2))
        else:
            back = 2 * n - 2 - k
            if back < 0 and after:
                self.got = hold(self.got, after, present, cost)
            self.mine.append(self.got)
            self.other.append(send(self.got, self.core))
            if back >= 0:
                whole, self.mark = join(self.mine, after, present, cost)
                self.got = send(whole, step_route(self.rows, self.seq, back))

    @property
    def count(self):
        return 2 * self.steps


def place_parts(number, groups, wide, piece, half):
    core = number[0]
    for group, (top, low) in enumerate(((core, number[1]), (1 - core, number[2]))):
        position = 0
        for part in groups[group]:
            for t in range(part.shape[0] // piece):
                start = pl.multiple_of((((position + t) ^ low) + top * half) * piece, 16)
                wide[pl.ds(start, piece)] = part[t * piece : (t + 1) * piece].astype(f32)
            position += part.shape[0] // piece


CHUNK = 256


def finish_kernel(number, *refs, specs, half, moves, smalls, came):
    refs = list(refs)

    def take(count):
        head = refs[:count]
        del refs[:count]
        return head

    groups = [(take(spec["parts"]), take(spec["parts"])) for spec in specs]
    small = take(1)[0] if smalls else None
    came = take(came)
    sums = [take(len(spec["layout"])) for spec in specs]
    small_out, move_out, (token,) = take(len(smalls)), take(len(moves)), take(1)
    wides, (both, out_sems) = take(len(specs)), take(2)
    copies = []

    def out(source, target):
        copies.append(pltpu.make_async_copy(source, target, out_sems.at[len(copies)]))
        copies[-1].start()

    for spec, group, wide, targets in zip(specs, groups, wides, sums, strict=True):
        place_parts(number, group, wide, spec["piece"], half)
        row = 0
        for target, blocks in zip(targets, spec["layout"], strict=True):
            for to_row, to_column, count in blocks:
                for c in range(0, count, CHUNK):
                    out(
                        wide.at[pl.ds(row + c, CHUNK)],
                        target.at[pl.ds(to_row + c, CHUNK), pl.ds(to_column, wide.shape[1])],
                    )
                row = row + count
    for pieces, target in zip(moves, move_out, strict=True):
        for i, row, rows, column in pieces:
            out(came[i].at[pl.ds(row, rows)], target.at[:, pl.ds(column, came[i].shape[1])])
    if smalls:
        count = groups[-1][0][0].shape[0]
        small_far = groups[-1][1][0][count:]
        both[...] = 0.5 * (small[...].astype(f32) + small_far.astype(f32))
        for (first, count), target in zip(smalls, small_out, strict=True):
            for i in range(count):
                width = both.shape[1]
                out(both.at[pl.ds(first + i, 1)], target.at[:, pl.ds(i * width, width)])
    token[...] = jnp.zeros_like(token)
    for copy in copies:
        copy.wait()


def finish(number, items, half, came=(), moves=(), smalls=(), after=(), present=()):
    width = items[0]["chain"].mine[0].shape[1]
    hbm = pl.BlockSpec(memory_space=pltpu.HBM)
    vmem = pl.BlockSpec(memory_space=pltpu.VMEM)
    specs = [
        dict(parts=len(item["chain"].mine), piece=item["piece"], layout=item["layout"])
        for item in items
    ]
    given = [part for item in items for part in item["chain"].mine + item["chain"].other]
    given += ([items[-1]["chain"].small] if smalls else []) + list(came)
    shapes = [s for item in items for s in item["shapes"]]
    wides = [pltpu.VMEM((2 * half * item["piece"], width), f32) for item in items]
    count = sum(w.shape[0] for w in wides) // CHUNK
    count += sum(len(m) for m in moves) + sum(n for _, n in smalls)
    moved = [jax.ShapeDtypeStruct((m[0][2], len(m) * width), bf16) for m in moves]

    def kernel(number, *refs):
        skip = len(after) + len(present)
        finish_kernel(
            number, *refs[: len(given)], *refs[len(given) + skip :],
            specs=specs, half=half, moves=moves, smalls=smalls, came=len(came),
        )

    res = pl.pallas_call(
        kernel,
        in_specs=[pl.BlockSpec(memory_space=pltpu.SMEM)]
        + [vmem] * (len(given) + len(after)) + [hbm] * len(present),
        out_specs=[hbm] * (len(shapes) + len(smalls) + len(moves)) + [vmem],
        out_shape=[jax.ShapeDtypeStruct(s, f32) for s in shapes]
        + [jax.ShapeDtypeStruct((1, n * width), f32) for _, n in smalls]
        + moved + [TOKEN],
        scratch_shapes=wides + [
            pltpu.VMEM((SMALL_ROWS, width), f32),
            pltpu.SemaphoreType.DMA((count,)),
        ],
        compiler_params=pltpu.CompilerParams(vmem_limit_bytes=36 * MIB),
        cost_estimate=taking(6),
    )(number, *given, *after, *present)
    return res[:-1], res[-1]


def pack(inputs, target, source, vectors):
    length, width = inputs.shape
    count = sum(v.shape[1] // width for v in vectors)
    outs = [
        jax.ShapeDtypeStruct((length + 16, width), bf16), jax.ShapeDtypeStruct((count, width), f32)
    ]

    def kernel(given, target, source, *refs):
        out, stacked = refs[-2:]
        out[:length] = given[...]
        out[length:] = jnp.zeros_like(out[length:])
        labels = jnp.concatenate([target[...], source[...]], axis=0)
        out[length : length + 2, :length] = labels.astype(f32).astype(bf16)
        row = 0
        for vector in refs[:-2]:
            for c in range(vector.shape[1] // width):
                stacked[row : row + 1] = vector[:, c * width : (c + 1) * width]
                row += 1

    args = [inputs, target, source, *vectors]
    return call(kernel, outs, args, lazy=range(len(args)), cost=2, limit=60)


def piece_rows(count, pieces):
    return -(-count // (pieces * 16)) * 16


def shards(
    inputs, memory, target_segments, memory_segments, self_project, self_query_bias,
    self_value_bias, self_output, self_output_bias, self_norm_gain, self_norm_bias, cross_query,
    cross_query_bias, cross_output, cross_output_bias, cross_norm_gain, cross_norm_bias,
    expand_weight, expand_bias, contract_weight, contract_bias, final_norm_gain, final_norm_bias,
    cotangent,
):
    rows, seq = lax.axis_size("rows"), lax.axis_size("seq")
    r, z = lax.axis_index("rows"), lax.axis_index("seq")
    _, length, width = inputs.shape
    hidden = expand_weight.shape[1]
    factor = float(width // HEADS) ** (-0.5)
    home = home_route(rows, seq)
    core = [(a * seq + b, (a ^ 1) * seq + b) for a in range(rows) for b in range(seq)]
    side = [(a * seq + b, a * seq + (b ^ 1)) for a in range(rows) for b in range(seq)]
    orders = bit_orders(rows)
    half = 2 ** (len(orders[0]) - 1)
    lows = [low_number(rows, order[:-1], r, z) for order in orders]
    is_one = (r & 1) == 1
    place = (z & 1) + 2 * (r & 1)
    number = jnp.stack([
        r & 1, jnp.where(is_one, lows[1], lows[0]), jnp.where(is_one, lows[0], lows[1]), place,
    ]).astype(jnp.int32)

    def line(vector):
        return vector.reshape(1, -1)

    m0 = send(memory[0], home)
    (packed, vectors), tick = pack(
        inputs[0], target_segments, memory_segments,
        [
            line(v)
            for v in (
                self_query_bias, self_value_bias, self_output_bias, self_norm_gain,
                self_norm_bias, cross_query_bias, cross_output_bias, cross_norm_gain,
                cross_norm_bias, contract_bias, final_norm_gain, final_norm_bias, expand_bias,
            )
        ],
    )
    x0 = send(packed, home)
    _, tick = call(lambda: None, [], [], cost=30, after=(tick,), limit=1)
    m0 = hold(m0, cost=20)
    x1 = send(x0, side)
    x2 = send(x0, core)
    m1 = send(m0, side)
    m2 = send(m0, core)
    x3 = send(x1, core)
    pulled = send(cotangent[0], home)

    def shape(*dims, dtype=f32):
        return jax.ShapeDtypeStruct(dims, dtype)

    def low(*dims):
        return jax.ShapeDtypeStruct(dims, bf16)

    vmem = pl.BlockSpec(memory_space=pltpu.VMEM)
    any_space = pl.BlockSpec(memory_space=pl.ANY)
    bias_space = pltpu.VMEM((length, 4 * length), f32)
    bias_turned = pltpu.VMEM((4 * length, length), f32)

    (pairs, query, self_result, self_logs, normed1, scale1, asked, marks), token = call(
        functools.partial(self_kernel, factor=factor),
        [
            low(4 * length, 2 * width), low(length, width), shape(length, width),
            shape(length, PAIR), shape(length, width), shape(length, PAIR), low(length, width),
            shape(8, 4 * length),
        ],
        [number[3:4], x0, x1, x2, x3, self_project, self_output, cross_query, vectors],
        scratch=[bias_space],
        lazy=[5, 8, 1, 2, 3, 4, 6, 7],
        cost=9,
        after=(tick,),
    )

    m1 = hold(m1, (), cost=20)
    m3 = send(m1, core)

    piece_a = piece_rows(hidden, 2 * half)
    piece_b = piece_rows(hidden + width, 2 * half)
    (
        output, keep_a, away_a, keep_b, away_b, small, cross_delta, crossed_pull, cross_result,
        cross_logs,
    ), _ = call(
        functools.partial(cross_kernel, factor=factor, piece_a=piece_a, piece_b=piece_b),
        [
            low(length, width), low(half * piece_a, width), low(half * piece_a, width),
            low(half * piece_b, width), low(half * piece_b, width),
            shape(SMALL_ROWS, width), shape(length, width), low(length, width),
            shape(length, width), shape(length, PAIR),
        ],
        [
            number, asked, m0, m1, m2, m3, marks, normed1, cross_output, expand_weight,
            contract_weight, vectors, pulled,
        ],
        scratch=[
            bias_space,
            pltpu.VMEM((2 * half * piece_a, width), bf16),
            pltpu.VMEM((2 * half * piece_b, width), bf16),
        ],
        lazy=[2, 3, 4, 5, 8, 9, 10, 12],
        cost=15,
        limit=44,
    )
    chains = {
        "A": Chain(keep_a, away_a, None, rows, seq),
        "B": Chain(keep_b, away_b, None, rows, seq),
    }

    (mem_near0, mem_near1, mem_far, asked_low), token = call(
        functools.partial(cross_back_kernel, factor=factor),
        [low(2 * length, width), low(2 * length, width), low(4 * length, width),
         low(length, width)],
        [asked, m0, m1, m2, m3, marks, crossed_pull, cross_result, cross_logs],
        scratch=[bias_turned],
        lazy=range(1, 5),
        cost=8,
    )
    for name in "AB":
        chains[name].step((token,))
        token = chains[name].mark
    mem_far = send(mem_far, core)

    (late, self_delta, mixed_pull, small), token = call(
        middle_kernel,
        [low(2 * width, width), shape(length, width), low(length, width),
         shape(SMALL_ROWS, width)],
        [
            asked_low, cross_delta, normed1, scale1, vectors, self_result, cross_query,
            self_output, small,
        ],
        lazy=[6, 7],
        cost=3,
        after=(token,),
    )
    onward, token = add_rows([(mem_near1, 0), (mem_far, 2 * length)], 2 * length, (token,))
    mem_got = send(onward, side)

    (dpairs, query_low), token = call(
        functools.partial(self_back_kernel, factor=factor),
        [low(4 * length, 2 * width), low(length, width)],
        [number[3:4], query, pairs, marks, mixed_pull, self_result, self_logs],
        scratch=[bias_turned],
        cost=8,
        after=(token,),
    )
    chains["A"].step((token,), (mem_got,) if SIDE == "A" else (), cost=SMALL_COST)
    late_piece = piece_rows(5 * width, 2 * half)
    (late_keep, late_away), token = call(
        functools.partial(project_sums_kernel, piece=late_piece),
        [low(half * late_piece, width), low(half * late_piece + SMALL_ROWS, width)],
        [number, dpairs, query_low, x0, x1, x2, x3, late, small],
        scratch=[
            pltpu.VMEM((2 * half * late_piece, width), bf16),
            pltpu.VMEM((width, 4 * length), bf16),
        ],
        lazy=range(3, 7),
        cost=K4B,
        after=(chains["A"].mark,),
    )
    chains["B"].step((token,), (mem_got,) if SIDE == "B" else (), cost=SMALL_COST)
    (in_near0, in_near1, in_far, base), token = call(
        project_back_kernel,
        [low(length, width), low(length, width), low(2 * length, width), shape(length, width)],
        [dpairs, query_low, self_delta, self_project],
        lazy=[3],
        cost=3,
        after=(chains["B"].mark,),
    )
    chains["L"] = Chain(late_keep, late_away, late_away[-SMALL_ROWS:], rows, seq)
    in_far = send(in_far, core)

    steps = " ".join(ORDER).split()
    blocks = range(hidden // width)
    smalls = [(0, 1), (1, 1), (2, 1), (3, 1), (4, 1), (5, 1), (6, hidden // width)]
    smalls += [(i, 1) for i in range(10, 16)]
    home_parts = [
        [(0, 0, length, 0)], [(0, length, length, 0), (0, 2 * length, length, width)]
    ]
    ends = {
        "A": dict(piece=piece_a, shapes=[(hidden, width)],
                  layout=[[(c * width, 0, width) for c in blocks]]),
        "B": dict(piece=piece_b, shapes=[(width, hidden), (width, width)],
                  layout=[[(0, c * width, width) for c in blocks], [(0, 0, width)]]),
        "L": dict(piece=late_piece, shapes=[(width, width), (width, width), (width, 3 * width)],
                  layout=[[(0, 0, width)], [(0, 0, width)],
                          [(0, c * width, width) for c in range(3)]]),
    }
    moves = home_parts + [[(1, 0, length, 0)]]
    known, done = {}, {}
    for step in steps:
        name, *wanted = step.split("+")
        cost = 0.1 if name.endswith("~") else FOLD
        name = name.rstrip("~")
        present = tuple(chains[w].got if w in chains else known[w] for w in wanted)
        if name in chains:
            chains[name].step((token,), present, cost=cost)
            token = chains[name].mark
        elif name == "m":
            known["m"], token = add_rows(
                [(mem_near0, 0), (mem_far, 0), (mem_got, 0)], 2 * length, (token,), present,
                front=output,
            )
            known["m"] = send(known["m"], home)
        elif name == "o":
            known["o"] = send(output, home)
        elif name in ("k", "v"):
            row = 0 if name == "k" else length
            known[name], token = add_rows(
                [(mem_near0, row), (mem_far, row), (mem_got, row)], length, (token,), present
            )
            known[name] = send(known[name], home)
        elif name == "x":
            onward, token = add_rows([(in_near1, 0), (in_far, length)], length, (token,), present)
            in_got = send(onward, side)
        elif name == "i":
            known["i"], token = add_rows(
                [(base, 0), (in_near0, 0), (in_far, 0), (in_got, 0)], length, (token,), present
            )
            known["i"] = send(known["i"], home)
        else:
            items = [dict(ends[c], chain=chains[c]) for c in name[1:]]
            last = "L" in name
            done[name[1:]], token = finish(
                number, items, half, after=(token,), present=present,
                came=[known["m"], known["i"]] if last else (), moves=moves if last else (),
                smalls=smalls if last else (),
            )
    (gradient_contract,) = done["A"]
    (
        gradient_expand, gradient_cross_output,
        gradient_cross_query, gradient_self_output, gradient_self_project, gradient_final_gain,
        gradient_final_bias, gradient_contract_bias, gradient_cross_gain, gradient_cross_bias,
        gradient_cross_output_bias, gradient_expand_bias, gradient_cross_query_bias,
        gradient_self_gain, gradient_self_bias, gradient_self_output_bias, gradient_query_bias,
        gradient_value_bias, output, memory_gradient, input_gradient,
    ) = done["BL"]

    return (
        output[None],
        input_gradient[None],
        memory_gradient[None],
        gradient_self_project,
        gradient_query_bias.reshape(-1),
        gradient_value_bias.reshape(-1),
        gradient_self_output,
        gradient_self_output_bias.reshape(-1),
        gradient_self_gain.reshape(-1),
        gradient_self_bias.reshape(-1),
        gradient_cross_query,
        gradient_cross_query_bias.reshape(-1),
        gradient_cross_output,
        gradient_cross_output_bias.reshape(-1),
        gradient_cross_gain.reshape(-1),
        gradient_cross_bias.reshape(-1),
        gradient_expand,
        gradient_expand_bias.reshape(-1),
        gradient_contract,
        gradient_contract_bias.reshape(-1),
        gradient_final_gain.reshape(-1),
        gradient_final_bias.reshape(-1),
    )


def solution(mesh):
    tokens = P("rows", "seq", None)
    in_specs = (tokens, tokens, P("rows", "seq"), P("rows", "seq")) + (P(),) * 19 + (tokens,)
    out_specs = (tokens,) * 3 + (P(),) * 19
    return jax.shard_map(shards, mesh=mesh, in_specs=in_specs, out_specs=out_specs, check_vma=False)
```

```python
import functools

import jax
import jax.numpy as jnp
from jax import lax
from jax.experimental import pallas as pl
from jax.experimental.pallas import tpu as pltpu
from jax.sharding import PartitionSpec as P

HEADS = 8
PAIR = 128
SMALL_ROWS = 16
masked_score = -1e30
epsilon = 1e-05
f32 = jnp.float32
bf16 = jnp.bfloat16
BOTH = ("rows", "seq")


def dot(left, right):
    return jnp.dot(left, right, preferred_element_type=f32)


def dot_nt(left, right):
    return lax.dot_general(left, right, (((1,), (1,)), ((), ())), preferred_element_type=f32)


def dot_tn(left, right):
    return lax.dot_general(left, right, (((0,), (0,)), ((), ())), preferred_element_type=f32)


def norm_forward(value, gain, shift):
    center = jnp.mean(value, axis=-1, keepdims=True)
    centred = value - center
    scale = lax.rsqrt(jnp.mean(centred * centred, axis=-1, keepdims=True) + epsilon)
    normed = centred * scale
    return normed * gain + shift, normed, scale


def norm_backward(incoming, normed, scale, gain):
    weighted = incoming * gain
    spread = weighted - jnp.mean(weighted, axis=-1, keepdims=True)
    spread = spread - normed * jnp.mean(weighted * normed, axis=-1, keepdims=True)
    return scale * spread, column_total(incoming * normed), column_total(incoming)


def column_total(value):
    return jnp.sum(value.astype(f32), axis=0, keepdims=True)


def head_lanes(shape, h):
    lane = lax.broadcasted_iota(jnp.int32, shape, 1)
    return (lane < 64) if h == 0 else (lane >= 64)


def only_head(value, h):
    return jnp.where(head_lanes(value.shape, h), value, jnp.zeros_like(value))


def flat_pairs(rows, seq, partner):
    return [(r * seq + z, partner(r, z)) for r in range(rows) for z in range(seq)]


def home_route(rows, seq):
    def partner(r, z):
        if (r & 1) == z // 2:
            return r * seq + z
        return (r ^ 1) * seq + (z ^ 2)

    return flat_pairs(rows, seq, partner)


def bit_orders(rows):
    count = rows.bit_length() - 2
    bits = [("r", 1 << (k + 1)) for k in range(count)]
    tail = [("z", 1), ("z", 2)]
    return bits + tail, bits[::-1] + tail


def step_route(rows, seq, k):
    orders = bit_orders(rows)

    def partner(r, z):
        kind, mask = orders[r & 1][k]
        return (r ^ mask) * seq + z if kind == "r" else r * seq + (z ^ mask)

    return flat_pairs(rows, seq, partner)


def low_number(rows, order, r, z):
    number = jnp.int32(0)
    for kind, mask in order:
        bit = jnp.where(((r if kind == "r" else z) & mask) != 0, 1, 0)
        number = number * 2 + bit
    return number


def send(value, route):
    return lax.ppermute(value, BOTH, route)


def taking(us):
    return pl.CostEstimate(
        flops=int(us * 1.15e9), bytes_accessed=int(us * 3.6e6), transcendentals=0
    )


class Lazy:
    def __init__(self, far, near, sem):
        self.copy, self.near, self.waiting = pltpu.make_async_copy(far, near, sem), near, True
        self.copy.start()

    @property
    def shape(self):
        return self.near.shape

    def __getitem__(self, index):
        if self.waiting:
            self.copy.wait()
            self.waiting = False
        return self.near[index]


TOKEN = jax.ShapeDtypeStruct((8, 128), f32)


def call(kernel, outs, args, scratch=(), lazy=(), out_specs=None, cost=None, after=(), present=(),
         limit=24):
    vmem = pl.BlockSpec(memory_space=pltpu.VMEM)
    smem = pl.BlockSpec(memory_space=pltpu.SMEM)
    hbm = pl.BlockSpec(memory_space=pltpu.HBM)
    count = len(args)
    lazy = list(lazy)

    def spec(i, arg):
        if i in lazy:
            return hbm
        return smem if arg.dtype == jnp.int32 and arg.ndim == 1 else vmem

    def inner(*refs):
        given = list(refs[:count])
        rest = refs[count + len(after) + len(present) :]
        results, token, held = rest[: len(outs)], rest[len(outs)], rest[len(outs) + 1 :]
        near, held = held[: len(lazy)], held[len(lazy) :]
        if lazy:
            sems, held = held[0], held[1:]
            for k, i in enumerate(lazy):
                given[i] = Lazy(given[i], near[k], sems.at[k])
        kernel(*given, *results, *held)
        for i in lazy:
            if given[i].waiting:
                given[i].copy.wait()
        token[...] = jnp.zeros_like(token)

    spaces = [pltpu.VMEM(args[i].shape, args[i].dtype) for i in lazy]
    if lazy:
        spaces.append(pltpu.SemaphoreType.DMA((len(lazy),)))
    res = pl.pallas_call(
        inner,
        out_shape=list(outs) + [TOKEN],
        in_specs=[spec(i, a) for i, a in enumerate(args)]
        + [vmem] * len(after) + [hbm] * len(present),
        out_specs=(out_specs if out_specs is not None else [vmem] * len(outs)) + [vmem],
        scratch_shapes=spaces + list(scratch),
        compiler_params=pltpu.CompilerParams(vmem_limit_bytes=limit * 1024 * 1024),
        cost_estimate=None if cost is None else taking(cost),
    )(*args, *after, *present)
    return res[:-1], res[-1]


def mask_bias(bias, place, query_labels, key_labels, length, causal):
    asking = jnp.broadcast_to(query_labels, (length, length)).T
    for s in range(4):
        same = asking == key_labels[s]
        if causal:
            query = place * length + lax.broadcasted_iota(jnp.int32, (length, length), 0)
            key = (place ^ s) * length + lax.broadcasted_iota(jnp.int32, (length, length), 1)
            same = same & (key <= query)
        bias[:, s * length : (s + 1) * length] = jnp.where(same, 0.0, masked_score)


def attend(query, keys, values, bias, factor, result, logs):
    length, width = query.shape
    lane = lax.broadcasted_iota(jnp.int32, (length, PAIR), 1)
    log_all = jnp.zeros((length, PAIR), f32)
    for j in range(width // PAIR):
        columns = slice(j * PAIR, (j + 1) * PAIR)
        pair = query[:, columns] * jnp.asarray(factor, bf16)
        key, value = keys(j), values(j)
        value = jnp.concatenate([value, jnp.ones_like(value)], axis=1)
        halves = []
        for h in range(2):
            scores = dot_nt(only_head(pair, h), key) + bias[...]
            peak = jnp.max(scores, axis=-1, keepdims=True)
            both = dot(jnp.exp(scores - peak).astype(bf16), value)
            total = both[:, PAIR:]
            halves.append(both[:, :PAIR] / total)
            log_all = jnp.where(lane == 2 * j + h, peak + jnp.log(total), log_all)
        result[:, columns] = jnp.where(lane < 64, halves[0], halves[1])
    logs[...] = log_all


def head_rows(query, result, pull, length, width):
    lane = lax.broadcasted_iota(jnp.int32, (length, PAIR), 1)
    sums = jnp.zeros((length, PAIR), f32)
    for j in range(width // PAIR):
        columns = slice(j * PAIR, (j + 1) * PAIR)
        product = pull[:, columns].astype(f32) * result[:, columns]
        for h in range(2):
            total = jnp.sum(only_head(product, h), axis=-1, keepdims=True)
            sums = jnp.where(lane == 2 * j + h, total, sums)
    return sums.T


def mask_bias_turned(bias, place, query_labels, key_labels, length, causal):
    for s in range(4):
        holding = jnp.broadcast_to(key_labels[s], (length, length)).T
        same = holding == query_labels
        if causal:
            query = place * length + lax.broadcasted_iota(jnp.int32, (length, length), 1)
            key = (place ^ s) * length + lax.broadcasted_iota(jnp.int32, (length, length), 0)
            same = same & (key <= query)
        bias[s * length : (s + 1) * length] = jnp.where(same, 0.0, masked_score)


def attend_back(query, keys, values, bias, factor, result, logs, pull, dq, store):
    length, width = query.shape
    deltas = head_rows(query, result, pull, length, width)
    totals = logs[...].T
    for j in range(width // PAIR):
        columns = slice(j * PAIR, (j + 1) * PAIR)
        pair = query[:, columns] * jnp.asarray(factor, bf16)
        wanted = pull[:, columns]
        key, value = keys(j), values(j)
        key_turned = key.T
        dkey, dvalue, dquery = 0.0, 0.0, []
        for h in range(2):
            row = slice(2 * j + h, 2 * j + h + 1)
            asking, pulling = only_head(pair, h), only_head(wanted, h)
            chance = jnp.exp(dot_nt(key, asking) + bias[...] - totals[row])
            slope = (chance * (dot_nt(value, pulling) - deltas[row])).astype(bf16)
            dquery.append(dot(key_turned[h * 64 : h * 64 + 64], slope))
            dkey = dkey + dot(slope, asking)
            dvalue = dvalue + dot(chance.astype(bf16), pulling)
        dq[:, columns] = (jnp.concatenate(dquery, axis=0).T * factor).astype(bf16)
        store(j, dkey.astype(bf16), dvalue.astype(bf16))


def rows_of(vectors, first, count):
    return [vectors[i : i + 1] for i in range(first, first + count)]


def row_labels(marks, row, length):
    return [marks[row : row + 1, s * length : (s + 1) * length] for s in range(4)]


def self_kernel(
    place, x0, x1, x2, x3, weight, out_weight, ask_weight, vectors,
    pairs, query, result, logs, normed, scale, asked, marks, bias, factor,
):
    length, width = query.shape
    blocks = (x0, x1, x2, x3)
    query_bias, value_bias, out_bias, gain, shift, ask_bias = rows_of(vectors, 0, 6)
    for s, block in enumerate(blocks):
        both = dot(block[:length], weight[:, width:])
        rows = slice(s * length, (s + 1) * length)
        pairs[rows, :width] = both[:, :width].astype(bf16)
        pairs[rows, width:] = (both[:, width:] + value_bias).astype(bf16)
    query[...] = (dot(x0[:length], weight[:, :width]) + query_bias).astype(bf16)
    for s, block in enumerate(blocks):
        columns = slice(s * length, (s + 1) * length)
        marks[:, columns] = block[length : length + 8, :length].astype(f32)
    labels = row_labels(marks, 0, length)
    mask_bias(bias, place[0], labels[0], labels, length, True)
    attend(
        query,
        lambda j: pairs[:, j * PAIR : (j + 1) * PAIR],
        lambda j: pairs[:, width + j * PAIR : width + (j + 1) * PAIR],
        bias, factor, result, logs,
    )
    mixed = result[...].astype(bf16)
    before = x0[:length].astype(f32) + dot(mixed, out_weight[...]) + out_bias
    first, normed[...], spread = norm_forward(before, gain, shift)
    scale[...] = jnp.broadcast_to(spread, scale.shape)
    asked[...] = (dot(first.astype(bf16), ask_weight[...]) + ask_bias).astype(bf16)


def memory_views(blocks, length, width):
    def keys(j):
        return jnp.concatenate([m[:length, j * PAIR : (j + 1) * PAIR] for m in blocks], axis=0)

    def values(j):
        return jnp.concatenate(
            [m[:length, width + j * PAIR : width + (j + 1) * PAIR] for m in blocks], axis=0
        )

    return keys, values


def cross_kernel(
    number, asked, m0, m1, m2, m3, marks, normed1, out_weight, grow, shrink, vectors, cotangent,
    output, keep_a, away_a, keep_b, away_b, small, delta, pull, result, logs,
    bias, sums_a, sums_b, factor, piece_a, piece_b,
):
    length, width = asked.shape
    hidden = grow.shape[1]
    blocks = (m0, m1, m2, m3)
    gain1, shift1 = rows_of(vectors, 3, 2)
    out_bias, gain2, shift2, shrink_bias, gain3, shift3 = rows_of(vectors, 6, 6)
    grow_bias = jnp.concatenate(rows_of(vectors, 12, hidden // width), axis=1)
    asking, labels = row_labels(marks, 0, length)[0], row_labels(marks, 1, length)
    mask_bias(bias, None, asking, labels, length, False)
    keys, values = memory_views(blocks, length, width)
    attend(asked, keys, values, bias, factor, result, logs)
    crossed = result[...].astype(bf16)
    first = normed1[...] * gain1 + shift1
    before = first + dot(crossed, out_weight[...]) + out_bias
    second, normed2, scale2 = norm_forward(before, gain2, shift2)
    second_low = second.astype(bf16)
    inner = dot(second_low, grow[...]) + grow_bias
    gate = 1.0 / (1.0 + jnp.exp(-inner))
    active = (inner * gate).astype(bf16)
    before = second + dot(active, shrink[...]) + shrink_bias
    final, normed3, scale3 = norm_forward(before, gain3, shift3)
    output[...] = final.astype(bf16)

    incoming = cotangent[...].astype(f32)
    third, gain3_sum, shift3_sum = norm_backward(incoming, normed3, scale3, gain3)
    shrink_low = third.astype(bf16)
    sums_a[0:hidden] = dot_tn(active, shrink_low).astype(bf16)
    fill_up(sums_a, hidden)
    slope = gate * (1.0 + inner * (1.0 - gate))
    grow_low = (dot_nt(shrink_low, shrink[...]) * slope).astype(bf16)
    grown = dot_tn(second_low, grow_low).astype(bf16)
    for c in range(hidden // width):
        sums_b[c * width : (c + 1) * width] = grown[:, c * width : (c + 1) * width]
    second_gradient = third + dot_nt(grow_low, grow[...])
    cross_delta, gain2_sum, shift2_sum = norm_backward(
        second_gradient, normed2, scale2, gain2
    )
    delta[...] = cross_delta
    cross_low = cross_delta.astype(bf16)
    sums_b[hidden : hidden + width] = dot_tn(crossed, cross_low).astype(bf16)
    fill_up(sums_b, hidden + width)
    spread_pieces(number, sums_a, keep_a, away_a, piece_a)
    spread_pieces(number, sums_b, keep_b, away_b, piece_b)
    pull[...] = dot_nt(cross_low, out_weight[...]).astype(bf16)
    grow_sum = column_total(grow_low)
    rows = [gain3_sum, shift3_sum, column_total(shrink_low), gain2_sum, shift2_sum,
            column_total(cross_low)]
    rows += [grow_sum[:, c * width : (c + 1) * width] for c in range(hidden // width)]
    rows += [jnp.zeros((SMALL_ROWS - len(rows), width), f32)]
    small[...] = jnp.concatenate(rows, axis=0)


def fill_up(sums, count):
    if sums.shape[0] > count:
        sums[count:] = jnp.zeros_like(sums[count:])


def spread_pieces(number, sums, keep, away, piece):
    half = sums.shape[0] // piece // 2
    core, mine, other = number[0], number[1], number[2]
    for q in range(half):
        for target, top, low in ((keep, core, mine), (away, 1 - core, other)):
            start = pl.multiple_of(((q ^ low) + top * half) * piece, 16)
            target[q * piece : (q + 1) * piece] = sums[pl.ds(start, piece)]


def cross_back_kernel(
    asked, m0, m1, m2, m3, marks, pull, result, logs, near0, near1, far, asked_low, bias, factor
):
    length, width = asked.shape
    blocks = (m0, m1, m2, m3)
    asking, labels = row_labels(marks, 0, length)[0], row_labels(marks, 1, length)
    mask_bias_turned(bias, None, asking, labels, length, False)
    keys, values = memory_views(blocks, length, width)
    outs = ((near0, 0), (near1, 0), (far, 0), (far, 2 * length))

    def store(j, dkey, dvalue):
        for k, part in enumerate((dkey, dvalue)):
            for s, (out, row) in enumerate(outs):
                start = row + k * length
                out[start : start + length, j * PAIR : (j + 1) * PAIR] = part[
                    s * length : (s + 1) * length
                ]

    attend_back(asked, keys, values, bias, factor, result, logs, pull, asked_low, store)


def middle_kernel(
    asked_low, cross_delta, normed1, scale1, vectors, self_result, ask_weight,
    self_out_weight, small_in, late, delta, mixed_pull, small,
):
    width = asked_low.shape[1]
    gain1, shift1 = rows_of(vectors, 3, 2)
    normed = normed1[...]
    first_low = (normed * gain1 + shift1).astype(bf16)
    first_gradient = cross_delta[...] + dot_nt(asked_low[...], ask_weight[...])
    self_delta, gain_sum, shift_sum = norm_backward(
        first_gradient, normed, scale1[:, 0:1], gain1
    )
    delta[...] = self_delta
    self_low = self_delta.astype(bf16)
    mixed_pull[...] = dot_nt(self_low, self_out_weight[...]).astype(bf16)
    late[0:width] = dot_tn(first_low, asked_low[...]).astype(bf16)
    late[width : 2 * width] = dot_tn(self_result[...].astype(bf16), self_low).astype(bf16)
    small[...] = small_in[...]
    small[10:14] = jnp.concatenate(
        [column_total(asked_low[...]), gain_sum, shift_sum, column_total(self_low)], axis=0
    )


def self_back_kernel(
    place, query, pairs, marks, pull, result, logs, dpairs, query_low, bias, factor
):
    length, width = query.shape
    labels = row_labels(marks, 0, length)
    mask_bias_turned(bias, place[0], labels[0], labels, length, True)

    def store(j, dkey, dvalue):
        dpairs[:, j * PAIR : (j + 1) * PAIR] = dkey
        dpairs[:, width + j * PAIR : width + (j + 1) * PAIR] = dvalue

    attend_back(
        query,
        lambda j: pairs[:, j * PAIR : (j + 1) * PAIR],
        lambda j: pairs[:, width + j * PAIR : width + (j + 1) * PAIR],
        bias, factor, result, logs, pull, query_low, store,
    )


def project_sums_kernel(
    number, dpairs, query_low, x0, x1, x2, x3, late, small_in,
    keep, away, sums, turned, piece,
):
    length, width = query_low.shape
    done = late.shape[0]
    sums[0:done] = late[...]
    for s, block in enumerate((x0, x1, x2, x3)):
        turned[:, s * length : (s + 1) * length] = block[:length].T
    sums[done : done + width] = dot(turned[:, :length], query_low[...]).astype(bf16)
    for half in range(2):
        total = dot(turned[...], dpairs[:, half * width : (half + 1) * width])
        sums[done + (1 + half) * width : done + (2 + half) * width] = total.astype(bf16)
    fill_up(sums, done + 3 * width)
    spread_pieces(number, sums, keep, away, piece)
    rows = keep.shape[0]
    sums_small = [column_total(query_low[...]), column_total(dpairs[:, width:])]
    whole = jnp.concatenate([small_in[:14]] + sums_small, axis=0)
    away[rows : rows + SMALL_ROWS] = whole.astype(bf16)


def project_back_kernel(dpairs, query_low, delta, weight, near0, near1, far, base):
    length, width = query_low.shape
    outs = (near0.at[...], near1.at[...], far.at[0:length], far.at[length : 2 * length])
    for s in range(4):
        outs[s][...] = dot_nt(dpairs[s * length : (s + 1) * length], weight[:, width:]).astype(bf16)
    base[...] = delta[...] + dot_nt(query_low[...], weight[:, :width])


def fold(keep, got, small, split, after, present=(), cost=30):
    count, width = keep.shape
    half = count // 2 if split else count
    extra = 0 if small is None else SMALL_ROWS
    args = [keep, got] + ([] if small is None else [small])
    outs = [jax.ShapeDtypeStruct((half, width), bf16)]
    separate = split or extra
    if separate:
        outs.append(jax.ShapeDtypeStruct((half + extra, width), bf16))
    if extra:
        outs.append(jax.ShapeDtypeStruct((SMALL_ROWS, width), bf16))

    def kernel(*refs):
        mine, other = refs[0], refs[1]
        results = list(refs[len(args) :])
        kept = (mine[:half].astype(f32) + other[:half].astype(f32)).astype(bf16)
        results.pop(0)[...] = kept
        onward = results.pop(0) if separate else None
        if split:
            onward[:half] = (
                mine[half:count].astype(f32) + other[half:count].astype(f32)
            ).astype(bf16)
        elif separate:
            onward[:half] = kept
        if extra:
            total = (refs[2][...].astype(f32) + other[count:].astype(f32)).astype(bf16)
            results.pop(0)[...] = total
            if separate:
                onward[half:] = total

    res, token = call(
        kernel, outs, args, after=after, present=present, cost=cost, limit=SMALL_LIMIT
    )
    res = list(res)
    kept = res.pop(0)
    onward = res.pop(0) if separate else kept
    return kept, onward, (res.pop(0) if extra else None), token


def add_rows(parts, rows, after, present=(), front=None):
    ahead = 0 if front is None else front.shape[0]

    def kernel(*refs):
        total = 0.0
        for (_, row), ref in zip(parts, refs, strict=False):
            total = total + ref[row : row + rows].astype(f32)
        if ahead:
            refs[-1][:ahead] = refs[len(parts)][...]
        refs[-1][ahead:] = total.astype(bf16)

    outs = [jax.ShapeDtypeStruct((ahead + rows, parts[0][0].shape[1]), bf16)]
    args = [a for a, _ in parts] + ([] if front is None else [front])
    (whole,), token = call(kernel, outs, args, after=after, present=present, cost=FOLD / 3,
                           limit=SMALL_LIMIT)
    return whole, token


def hold(value, after=(), present=(), cost=1):
    any_space = pl.BlockSpec(memory_space=pl.ANY)
    extra = [*after, *present]
    return pl.pallas_call(
        lambda *refs: None,
        out_shape=jax.ShapeDtypeStruct(value.shape, value.dtype),
        in_specs=[any_space] * (1 + len(extra)),
        out_specs=any_space,
        input_output_aliases={0: 0},
        compiler_params=pltpu.CompilerParams(vmem_limit_bytes=1024 * 1024),
        cost_estimate=taking(cost),
    )(value, *extra)


def join(parts, after, present=(), cost=30):
    count = sum(part.shape[0] for part in parts)

    def kernel(*refs):
        position = 0
        for part in refs[: len(parts)]:
            refs[-1][position : position + part.shape[0]] = part[...]
            position += part.shape[0]

    outs = [jax.ShapeDtypeStruct((count, parts[0].shape[1]), bf16)]
    (whole,), token = call(
        kernel, outs, list(parts), after=after, present=present, cost=cost,
        limit=SMALL_LIMIT,
    )
    return whole, token


ORDER = (
    "A L B x", "A~ B~ L A", "L i B A", "L A B L+i",
    "m B L A", "fA L B+L+i+m L", "fBL",
)
FOLD = 30
SMALL_LIMIT = 24
MIB = 1024 * 1024
SMALL_COST = 0.1
K4B = 0.1
SIDE = "B"


class Chain:
    def __init__(self, keep, away, small, rows, seq):
        self.rows, self.seq = rows, seq
        self.core = [(r * seq + z, (r ^ 1) * seq + z) for r in range(rows) for z in range(seq)]
        self.keep, self.small = keep, small
        self.got = send(away, self.core)
        self.steps = len(bit_orders(rows)[0])
        self.k = 0
        self.mark = None
        self.mine = self.other = None

    def step(self, after=(), present=(), cost=30):
        k, n = self.k, self.steps
        self.k += 1
        if k <= n:
            self.keep, onward, self.small, self.mark = fold(
                self.keep, self.got, self.small, k < n - 1, after, present, cost
            )
            if k < n:
                self.got = send(onward, step_route(self.rows, self.seq, k))
            else:
                self.mine, self.other = [self.keep], [send(onward, self.core)]
                self.got = send(self.keep, step_route(self.rows, self.seq, n - 2))
        else:
            back = 2 * n - 2 - k
            if back < 0 and after:
                self.got = hold(self.got, after, present, cost)
            self.mine.append(self.got)
            self.other.append(send(self.got, self.core))
            if back >= 0:
                whole, self.mark = join(self.mine, after, present, cost)
                self.got = send(whole, step_route(self.rows, self.seq, back))

    @property
    def count(self):
        return 2 * self.steps


def place_parts(number, groups, wide, piece, half):
    core = number[0]
    for group, (top, low) in enumerate(((core, number[1]), (1 - core, number[2]))):
        position = 0
        for part in groups[group]:
            for t in range(part.shape[0] // piece):
                start = pl.multiple_of((((position + t) ^ low) + top * half) * piece, 16)
                wide[pl.ds(start, piece)] = part[t * piece : (t + 1) * piece].astype(f32)
            position += part.shape[0] // piece


CHUNK = 256


def finish_kernel(number, *refs, specs, half, moves, smalls, came):
    refs = list(refs)

    def take(count):
        head = refs[:count]
        del refs[:count]
        return head

    groups = [(take(spec["parts"]), take(spec["parts"])) for spec in specs]
    small = take(1)[0] if smalls else None
    came = take(came)
    sums = [take(len(spec["layout"])) for spec in specs]
    small_out, move_out, (token,) = take(len(smalls)), take(len(moves)), take(1)
    wides, (both, out_sems) = take(len(specs)), take(2)
    copies = []

    def out(source, target):
        copies.append(pltpu.make_async_copy(source, target, out_sems.at[len(copies)]))
        copies[-1].start()

    for spec, group, wide, targets in zip(specs, groups, wides, sums, strict=True):
        place_parts(number, group, wide, spec["piece"], half)
        row = 0
        for target, blocks in zip(targets, spec["layout"], strict=True):
            for to_row, to_column, count in blocks:
                for c in range(0, count, CHUNK):
                    out(
                        wide.at[pl.ds(row + c, CHUNK)],
                        target.at[pl.ds(to_row + c, CHUNK), pl.ds(to_column, wide.shape[1])],
                    )
                row = row + count
    for pieces, target in zip(moves, move_out, strict=True):
        for i, row, rows, column in pieces:
            out(came[i].at[pl.ds(row, rows)], target.at[:, pl.ds(column, came[i].shape[1])])
    if smalls:
        count = groups[-1][0][0].shape[0]
        small_far = groups[-1][1][0][count:]
        both[...] = 0.5 * (small[...].astype(f32) + small_far.astype(f32))
        for (first, count), target in zip(smalls, small_out, strict=True):
            for i in range(count):
                width = both.shape[1]
                out(both.at[pl.ds(first + i, 1)], target.at[:, pl.ds(i * width, width)])
    token[...] = jnp.zeros_like(token)
    for copy in copies:
        copy.wait()


def finish(number, items, half, came=(), moves=(), smalls=(), after=(), present=()):
    width = items[0]["chain"].mine[0].shape[1]
    hbm = pl.BlockSpec(memory_space=pltpu.HBM)
    vmem = pl.BlockSpec(memory_space=pltpu.VMEM)
    specs = [
        dict(parts=len(item["chain"].mine), piece=item["piece"], layout=item["layout"])
        for item in items
    ]
    given = [part for item in items for part in item["chain"].mine + item["chain"].other]
    given += ([items[-1]["chain"].small] if smalls else []) + list(came)
    shapes = [s for item in items for s in item["shapes"]]
    wides = [pltpu.VMEM((2 * half * item["piece"], width), f32) for item in items]
    count = sum(w.shape[0] for w in wides) // CHUNK
    count += sum(len(m) for m in moves) + sum(n for _, n in smalls)
    moved = [jax.ShapeDtypeStruct((m[0][2], len(m) * width), bf16) for m in moves]

    def kernel(number, *refs):
        skip = len(after) + len(present)
        finish_kernel(
            number, *refs[: len(given)], *refs[len(given) + skip :],
            specs=specs, half=half, moves=moves, smalls=smalls, came=len(came),
        )

    res = pl.pallas_call(
        kernel,
        in_specs=[pl.BlockSpec(memory_space=pltpu.SMEM)]
        + [vmem] * (len(given) + len(after)) + [hbm] * len(present),
        out_specs=[hbm] * (len(shapes) + len(smalls) + len(moves)) + [vmem],
        out_shape=[jax.ShapeDtypeStruct(s, f32) for s in shapes]
        + [jax.ShapeDtypeStruct((1, n * width), f32) for _, n in smalls]
        + moved + [TOKEN],
        scratch_shapes=wides + [
            pltpu.VMEM((SMALL_ROWS, width), f32),
            pltpu.SemaphoreType.DMA((count,)),
        ],
        compiler_params=pltpu.CompilerParams(vmem_limit_bytes=36 * MIB),
        cost_estimate=taking(6),
    )(number, *given, *after, *present)
    return res[:-1], res[-1]


def pack(inputs, target, source, vectors):
    length, width = inputs.shape
    count = sum(v.shape[1] // width for v in vectors)
    outs = [
        jax.ShapeDtypeStruct((length + 16, width), bf16), jax.ShapeDtypeStruct((count, width), f32)
    ]

    def kernel(given, target, source, *refs):
        out, stacked = refs[-2:]
        out[:length] = given[...]
        out[length:] = jnp.zeros_like(out[length:])
        labels = jnp.concatenate([target[...], source[...]], axis=0)
        out[length : length + 2, :length] = labels.astype(f32).astype(bf16)
        row = 0
        for vector in refs[:-2]:
            for c in range(vector.shape[1] // width):
                stacked[row : row + 1] = vector[:, c * width : (c + 1) * width]
                row += 1

    args = [inputs, target, source, *vectors]
    return call(kernel, outs, args, lazy=range(len(args)), cost=2, limit=60)


def piece_rows(count, pieces):
    return -(-count // (pieces * 16)) * 16


def shards(
    inputs, memory, target_segments, memory_segments, self_project, self_query_bias,
    self_value_bias, self_output, self_output_bias, self_norm_gain, self_norm_bias, cross_query,
    cross_query_bias, cross_output, cross_output_bias, cross_norm_gain, cross_norm_bias,
    expand_weight, expand_bias, contract_weight, contract_bias, final_norm_gain, final_norm_bias,
    cotangent,
):
    rows, seq = lax.axis_size("rows"), lax.axis_size("seq")
    r, z = lax.axis_index("rows"), lax.axis_index("seq")
    _, length, width = inputs.shape
    hidden = expand_weight.shape[1]
    factor = float(width // HEADS) ** (-0.5)
    home = home_route(rows, seq)
    core = [(a * seq + b, (a ^ 1) * seq + b) for a in range(rows) for b in range(seq)]
    side = [(a * seq + b, a * seq + (b ^ 1)) for a in range(rows) for b in range(seq)]
    orders = bit_orders(rows)
    half = 2 ** (len(orders[0]) - 1)
    lows = [low_number(rows, order[:-1], r, z) for order in orders]
    is_one = (r & 1) == 1
    place = (z & 1) + 2 * (r & 1)
    number = jnp.stack([
        r & 1, jnp.where(is_one, lows[1], lows[0]), jnp.where(is_one, lows[0], lows[1]), place,
    ]).astype(jnp.int32)

    def line(vector):
        return vector.reshape(1, -1)

    m0 = send(memory[0], home)
    (packed, vectors), tick = pack(
        inputs[0], target_segments, memory_segments,
        [
            line(v)
            for v in (
                self_query_bias, self_value_bias, self_output_bias, self_norm_gain,
                self_norm_bias, cross_query_bias, cross_output_bias, cross_norm_gain,
                cross_norm_bias, contract_bias, final_norm_gain, final_norm_bias, expand_bias,
            )
        ],
    )
    x0 = send(packed, home)
    _, tick = call(lambda: None, [], [], cost=30, after=(tick,), limit=1)
    m0 = hold(m0, cost=20)
    x1 = send(x0, side)
    x2 = send(x0, core)
    m1 = send(m0, side)
    m2 = send(m0, core)
    x3 = send(x1, core)
    pulled = send(cotangent[0], home)

    def shape(*dims, dtype=f32):
        return jax.ShapeDtypeStruct(dims, dtype)

    def low(*dims):
        return jax.ShapeDtypeStruct(dims, bf16)

    vmem = pl.BlockSpec(memory_space=pltpu.VMEM)
    any_space = pl.BlockSpec(memory_space=pl.ANY)
    bias_space = pltpu.VMEM((length, 4 * length), f32)
    bias_turned = pltpu.VMEM((4 * length, length), f32)

    (pairs, query, self_result, self_logs, normed1, scale1, asked, marks), token = call(
        functools.partial(self_kernel, factor=factor),
        [
            low(4 * length, 2 * width), low(length, width), shape(length, width),
            shape(length, PAIR), shape(length, width), shape(length, PAIR), low(length, width),
            shape(8, 4 * length),
        ],
        [number[3:4], x0, x1, x2, x3, self_project, self_output, cross_query, vectors],
        scratch=[bias_space],
        lazy=[5, 8, 1, 2, 3, 4, 6, 7],
        cost=9,
        after=(tick,),
    )

    m1 = hold(m1, (), cost=20)
    m3 = send(m1, core)

    piece_a = piece_rows(hidden, 2 * half)
    piece_b = piece_rows(hidden + width, 2 * half)
    (
        output, keep_a, away_a, keep_b, away_b, small, cross_delta, crossed_pull, cross_result,
        cross_logs,
    ), _ = call(
        functools.partial(cross_kernel, factor=factor, piece_a=piece_a, piece_b=piece_b),
        [
            low(length, width), low(half * piece_a, width), low(half * piece_a, width),
            low(half * piece_b, width), low(half * piece_b, width),
            shape(SMALL_ROWS, width), shape(length, width), low(length, width),
            shape(length, width), shape(length, PAIR),
        ],
        [
            number, asked, m0, m1, m2, m3, marks, normed1, cross_output, expand_weight,
            contract_weight, vectors, pulled,
        ],
        scratch=[
            bias_space,
            pltpu.VMEM((2 * half * piece_a, width), bf16),
            pltpu.VMEM((2 * half * piece_b, width), bf16),
        ],
        lazy=[2, 3, 4, 5, 8, 9, 10, 12],
        cost=15,
        limit=44,
    )
    chains = {
        "A": Chain(keep_a, away_a, None, rows, seq),
        "B": Chain(keep_b, away_b, None, rows, seq),
    }

    (mem_near0, mem_near1, mem_far, asked_low), token = call(
        functools.partial(cross_back_kernel, factor=factor),
        [low(2 * length, width), low(2 * length, width), low(4 * length, width),
         low(length, width)],
        [asked, m0, m1, m2, m3, marks, crossed_pull, cross_result, cross_logs],
        scratch=[bias_turned],
        lazy=range(1, 5),
        cost=8,
    )
    for name in "AB":
        chains[name].step((token,))
        token = chains[name].mark
    mem_far = send(mem_far, core)

    (late, self_delta, mixed_pull, small), token = call(
        middle_kernel,
        [low(2 * width, width), shape(length, width), low(length, width),
         shape(SMALL_ROWS, width)],
        [
            asked_low, cross_delta, normed1, scale1, vectors, self_result, cross_query,
            self_output, small,
        ],
        lazy=[6, 7],
        cost=3,
        after=(token,),
    )
    onward, token = add_rows([(mem_near1, 0), (mem_far, 2 * length)], 2 * length, (token,))
    mem_got = send(onward, side)

    (dpairs, query_low), token = call(
        functools.partial(self_back_kernel, factor=factor),
        [low(4 * length, 2 * width), low(length, width)],
        [number[3:4], query, pairs, marks, mixed_pull, self_result, self_logs],
        scratch=[bias_turned],
        cost=8,
        after=(token,),
    )
    chains["A"].step((token,), (mem_got,) if SIDE == "A" else (), cost=SMALL_COST)
    late_piece = piece_rows(5 * width, 2 * half)
    (late_keep, late_away), token = call(
        functools.partial(project_sums_kernel, piece=late_piece),
        [low(half * late_piece, width), low(half * late_piece + SMALL_ROWS, width)],
        [number, dpairs, query_low, x0, x1, x2, x3, late, small],
        scratch=[
            pltpu.VMEM((2 * half * late_piece, width), bf16),
            pltpu.VMEM((width, 4 * length), bf16),
        ],
        lazy=range(3, 7),
        cost=K4B,
        after=(chains["A"].mark,),
    )
    chains["B"].step((token,), (mem_got,) if SIDE == "B" else (), cost=SMALL_COST)
    (in_near0, in_near1, in_far, base), token = call(
        project_back_kernel,
        [low(length, width), low(length, width), low(2 * length, width), shape(length, width)],
        [dpairs, query_low, self_delta, self_project],
        lazy=[3],
        cost=3,
        after=(chains["B"].mark,),
    )
    chains["L"] = Chain(late_keep, late_away, late_away[-SMALL_ROWS:], rows, seq)
    in_far = send(in_far, core)

    steps = " ".join(ORDER).split()
    blocks = range(hidden // width)
    smalls = [(0, 1), (1, 1), (2, 1), (3, 1), (4, 1), (5, 1), (6, hidden // width)]
    smalls += [(i, 1) for i in range(10, 16)]
    home_parts = [
        [(0, 0, length, 0)], [(0, length, length, 0), (0, 2 * length, length, width)]
    ]
    ends = {
        "A": dict(piece=piece_a, shapes=[(hidden, width)],
                  layout=[[(c * width, 0, width) for c in blocks]]),
        "B": dict(piece=piece_b, shapes=[(width, hidden), (width, width)],
                  layout=[[(0, c * width, width) for c in blocks], [(0, 0, width)]]),
        "L": dict(piece=late_piece, shapes=[(width, width), (width, width), (width, 3 * width)],
                  layout=[[(0, 0, width)], [(0, 0, width)],
                          [(0, c * width, width) for c in range(3)]]),
    }
    moves = home_parts + [[(1, 0, length, 0)]]
    known, done = {}, {}
    for step in steps:
        name, *wanted = step.split("+")
        cost = 0.1 if name.endswith("~") else FOLD
        name = name.rstrip("~")
        present = tuple(chains[w].got if w in chains else known[w] for w in wanted)
        if name in chains:
            chains[name].step((token,), present, cost=cost)
            token = chains[name].mark
        elif name == "m":
            known["m"], token = add_rows(
                [(mem_near0, 0), (mem_far, 0), (mem_got, 0)], 2 * length, (token,), present,
                front=output,
            )
            known["m"] = send(known["m"], home)
        elif name == "o":
            known["o"] = send(output, home)
        elif name in ("k", "v"):
            row = 0 if name == "k" else length
            known[name], token = add_rows(
                [(mem_near0, row), (mem_far, row), (mem_got, row)], length, (token,), present
            )
            known[name] = send(known[name], home)
        elif name == "x":
            onward, token = add_rows([(in_near1, 0), (in_far, length)], length, (token,), present)
            in_got = send(onward, side)
        elif name == "i":
            known["i"], token = add_rows(
                [(base, 0), (in_near0, 0), (in_far, 0), (in_got, 0)], length, (token,), present
            )
            known["i"] = send(known["i"], home)
        else:
            items = [dict(ends[c], chain=chains[c]) for c in name[1:]]
            last = "L" in name
            done[name[1:]], token = finish(
                number, items, half, after=(token,), present=present,
                came=[known["m"], known["i"]] if last else (), moves=moves if last else (),
                smalls=smalls if last else (),
            )
    (gradient_contract,) = done["A"]
    (
        gradient_expand, gradient_cross_output,
        gradient_cross_query, gradient_self_output, gradient_self_project, gradient_final_gain,
        gradient_final_bias, gradient_contract_bias, gradient_cross_gain, gradient_cross_bias,
        gradient_cross_output_bias, gradient_expand_bias, gradient_cross_query_bias,
        gradient_self_gain, gradient_self_bias, gradient_self_output_bias, gradient_query_bias,
        gradient_value_bias, output, memory_gradient, input_gradient,
    ) = done["BL"]

    return (
        output[None],
        input_gradient[None],
        memory_gradient[None],
        gradient_self_project,
        gradient_query_bias.reshape(-1),
        gradient_value_bias.reshape(-1),
        gradient_self_output,
        gradient_self_output_bias.reshape(-1),
        gradient_self_gain.reshape(-1),
        gradient_self_bias.reshape(-1),
        gradient_cross_query,
        gradient_cross_query_bias.reshape(-1),
        gradient_cross_output,
        gradient_cross_output_bias.reshape(-1),
        gradient_cross_gain.reshape(-1),
        gradient_cross_bias.reshape(-1),
        gradient_expand,
        gradient_expand_bias.reshape(-1),
        gradient_contract,
        gradient_contract_bias.reshape(-1),
        gradient_final_gain.reshape(-1),
        gradient_final_bias.reshape(-1),
    )


def solution(mesh):
    tokens = P("rows", "seq", None)
    in_specs = (tokens, tokens, P("rows", "seq"), P("rows", "seq")) + (P(),) * 19 + (tokens,)
    out_specs = (tokens,) * 3 + (P(),) * 19
    return jax.shard_map(shards, mesh=mesh, in_specs=in_specs, out_specs=out_specs, check_vma=False)
```
